512 devices in a mesh: grp: 16 (over y, core), ep: 32 (over z, x).
Axes of the slice: x: 4, y: 8, z: 8, core: 2. Of those that a mesh axis runs over, the one named last changes fastest.
Arguments:
- resp_q: bfloat16 [65536, 4096], P(('grp', 'ep')), may hold values from -6 to 6
- resp_kv: bfloat16 [65536, 512], P(('grp', 'ep')), may hold values from -96 to 96
- prompt_kv: bfloat16 [12288, 512], P(('grp', 'ep')), may hold values from -96 to 96
- moe_in: bfloat16 [65536, 2048], P(('grp', 'ep')), may hold values from -6 to 6
- routes: int32 [65536, 8], P(('grp', 'ep')), may hold values from 0 to 127, all different within a row; in each aligned block of 128 rows (0 to 127, 128 to 255, ...) at most 16 rows name the same one
- gate_probs: float32 [65536, 8], P(('grp', 'ep')), may hold values from 0.1 to 1
- w_gate: bfloat16 [32, 2048, 768], P('ep', 'grp'), may hold values from -0.125 to 0.125
- w_up: bfloat16 [32, 2048, 768], P('ep', 'grp'), may hold values from -0.125 to 0.125
- w_down: bfloat16 [32, 2048, 768], P('ep', 'grp'), may hold values from -0.21875 to 0.21875
Outputs:
- context: bfloat16 [65536, 4096], P(('grp', 'ep'))
- moe_out: bfloat16 [65536, 2048], P(('grp', 'ep'))
The draws below stay inside these ranges and needn't reach their ends.
Inputs may be any that keep to these rules, and one draw needn't show every extreme that they name: `routes`: each row names 8 different experts; within the 128 rows of one device no expert is named more than 16 times.
All inputs are finite; a program needn't handle non-finite values.
Results may differ from the reference program's by a relative error of at most 0.0057.
Values may be sent and summed in bfloat16 or wider, within the bound.
A program may use at most 64 MiB of HBM per device.

```python
import math
import jax
import jax.numpy as jnp
import numpy as np
from jax import lax

D = 2048
FF = 768
HQ = 32
KVH = 2
HD = 128
EXPERTS = 128
TOPK = 8
TOK_DEV = 128
CAP = 16
EXP_DEV = 4
PROMPT = 768
RESP_LEN = 128
RESPONSES = 32
GROUPS = 16
TOKENS = 65536
N_EP = 32


def draw_resp_q(key, part):
    key = jax.random.fold_in(key, 101)
    key_one = jax.random.fold_in(key, 0)
    full_shape = (TOKENS, KVH, HQ // KVH, HD)
    drawn = jnp.clip(jax.random.normal(key_one, full_shape, jnp.float32), -6.0, 6.0)
    return drawn.reshape(TOKENS, HQ * HD).astype(jnp.bfloat16)


def draw_prompt_kv(key, part):
    key = jax.random.fold_in(key, 202)
    key_one, key_two = jax.random.split(key, 2)
    row_count = GROUPS * PROMPT
    full_shape = (row_count, KVH, HD)
    key_part = jnp.clip(jax.random.normal(key_one, full_shape, jnp.float32), -6.0, 6.0)
    value_part = jnp.clip(jax.random.normal(key_two, full_shape, jnp.float32), -6.0, 6.0) * 16.0
    return jnp.stack([key_part, value_part], axis=1).reshape(row_count, 2 * KVH * HD).astype(jnp.bfloat16)


def draw_resp_kv(key, part):
    key = jax.random.fold_in(key, 303)
    key_one, key_two = jax.random.split(key, 2)
    full_shape = (TOKENS, KVH, HD)
    key_part = jnp.clip(jax.random.normal(key_one, full_shape, jnp.float32), -6.0, 6.0)
    value_part = jnp.clip(jax.random.normal(key_two, full_shape, jnp.float32), -6.0, 6.0) * 16.0
    return jnp.stack([key_part, value_part], axis=1).reshape(TOKENS, 2 * KVH * HD).astype(jnp.bfloat16)


def shard_levels(own_key, shape, cuts, low, largest):
    level, own = 1.0, jax.random.fold_in(own_key, 6)
    for dim, shards_of in cuts:
        steps = jnp.exp(jax.random.uniform(jax.random.fold_in(own, dim), (shards_of,), jnp.float32, low / len(cuts), largest / len(cuts)))
        level = level * jnp.repeat(steps, shape[dim] // shards_of).reshape([-1 if axis == dim else 1 for axis in range(len(shape))])
    return level


def shared_out(rng, own, number, rows, number_of, top, reach, skew):
    ranking = jax.random.permutation(rng, number_of)
    packed, common = shares(number_of, rows * top, reach, skew, True), shares(number_of, rows * top, reach, skew, False)
    places = jnp.arange(number_of)

    def named(lengths, turn):
        used = int((lengths > 0).sum())
        fixed = max(1, used // 4)
        moved = fixed + (places - fixed + turn * (used - fixed)) % max(1, number_of - fixed)
        return jnp.zeros((number_of,), jnp.int32).at[ranking[jnp.where(places < fixed, places, moved)]].set(jnp.asarray(lengths, jnp.int32))

    lengths = jnp.where(number % 4 == 0, named(packed, number // 4), named(common, number - number // 4 - 1))
    mixed = jax.random.permutation(jax.random.fold_in(own, 3), number_of)
    source_of, taker = mixed[0:number_of // 2 * 2:2], mixed[1:number_of // 2 * 2:2]
    slack = jnp.minimum(lengths[source_of] - 1, reach - lengths[taker]) // 2
    slack = jnp.where((source_of == ranking[0]) | (taker == ranking[0]) | (lengths[taker] == 0), 0, jnp.maximum(slack, 0))
    moved = jax.random.randint(jax.random.fold_in(own, 4), (number_of // 2,), 0, 1 << 20) % (slack + 1)
    lengths = lengths.at[source_of].add(-moved).at[taker].add(moved)
    items = jnp.searchsorted(jnp.cumsum(lengths), jnp.arange(rows * top), side="right").astype(jnp.int32)
    listing = items.reshape(top, rows).T
    listing = listing[jax.random.permutation(jax.random.fold_in(own, 1), rows)]
    turn = jax.random.randint(jax.random.fold_in(own, 2), (rows, 1), 0, top)
    return jnp.take_along_axis(listing, (jnp.arange(top)[None, :] + turn) % top, axis=1)


def shares(amount, total, most, lean, full):
    loads = [(1 << 20) // math.isqrt(rank ** lean) + 1 for rank in range(1, amount + 1)]
    largest = most if full else min(most, max(-(-total // amount), total * loads[0] // sum(loads)))
    least = 1 if total - largest >= amount - 1 else 0
    given, spare = [largest] + [least] * (amount - 1), total - largest - least * (amount - 1)
    while spare > 0:
        free = [i for i in range(1, amount) if given[i] < largest] or [i for i in range(1, amount) if given[i] < most]
        mass, left = sum([loads[i] for i in free]), spare
        for i in free:
            addition = min(most - given[i], max(1, left * loads[i] // mass), spare)
            given[i] = given[i] + addition
            spare = spare - addition
    return np.array(given)


def noise(stream_key, dims, scale, bound, shards=(), kind=jnp.bfloat16):
    gain = shard_levels(stream_key, dims, shards, -0.22, 0.18) if shards else 1.0
    array = jax.random.normal(stream_key, dims, jnp.float32) * scale * gain
    return jnp.minimum(jnp.maximum(array, -bound), bound).astype(kind)


def setup_inputs(seed: int = 0) -> dict:
    key_list = jax.random.split(jax.random.key(seed), 10)
    resp_q = draw_resp_q(jax.random.fold_in(key_list[9], 71), 0)
    resp_kv = draw_resp_kv(jax.random.fold_in(key_list[9], 71), 0)
    prompt_kv = draw_prompt_kv(jax.random.fold_in(key_list[9], 71), 0)
    moe_in = noise(key_list[3], (TOKENS, D), 1.0, 6.0, ((0, 512),))
    routes_keys = jax.random.split(jax.random.fold_in(key_list[4], 1), TOKENS // TOK_DEV)
    routes_turns = jax.random.permutation(jax.random.fold_in(key_list[4], 3), TOKENS // TOK_DEV)
    routes = jax.vmap(lambda own, number: shared_out(jax.random.fold_in(key_list[4], 2), own, number, TOK_DEV, EXPERTS, TOPK, CAP, 2))(routes_keys, routes_turns).reshape((TOKENS, TOPK))
    gate_probs = jnp.clip(jnp.exp(math.log(1.0) - 2.3025851 * jax.random.uniform(key_list[5], (TOKENS, TOPK), jnp.float32) ** shard_levels(key_list[5], (TOKENS, TOPK), ((0, 512),), -0.2, 0.2)), 0.1, 1.0)
    w_gate = noise(key_list[6], (N_EP, D, FF), D ** -0.5, 0.125, ((0, 32), (1, 16)))
    w_up = noise(key_list[7], (N_EP, D, FF), D ** -0.5, 0.125, ((0, 32), (1, 16)))
    w_down = noise(key_list[8], (N_EP, D, FF), FF ** -0.5, 0.21875, ((0, 32), (1, 16)))
    return dict(resp_q=resp_q, resp_kv=resp_kv, prompt_kv=prompt_kv, moe_in=moe_in, routes=routes, gate_probs=gate_probs, w_gate=w_gate, w_up=w_up, w_down=w_down)


def attend_response(resp_queries, resp_pairs, group_prompt):
    key_rows = jnp.concatenate([group_prompt[:, 0], resp_pairs[:, 0]], axis=0).astype(jnp.float32)
    value_rows = jnp.concatenate([group_prompt[:, 1], resp_pairs[:, 1]], axis=0).astype(jnp.float32)
    scores = jnp.einsum("lhgd,khd->hglk", resp_queries.astype(jnp.float32), key_rows) * (HD ** -0.5)
    query_pos = jnp.arange(RESP_LEN)[:, None]
    key_pos = jnp.arange(PROMPT + RESP_LEN)[None, :]
    visible = (key_pos < PROMPT) | (key_pos - PROMPT <= query_pos)
    scores = jnp.where(visible, scores, -jnp.inf)
    row_max = jnp.max(scores, axis=-1, keepdims=True)
    exp_scores = jnp.exp(scores - row_max)
    denominator = jnp.sum(exp_scores, axis=-1)
    rounded = lax.optimization_barrier(exp_scores.astype(jnp.bfloat16)).astype(jnp.float32)
    summed = jnp.einsum("hglk,khd->lhgd", rounded, value_rows)
    context = summed / jnp.transpose(denominator, (2, 0, 1))[..., None]
    return context.astype(jnp.bfloat16)


def slot_layout(route_rows):
    expert_range = jnp.arange(EXPERTS, dtype=jnp.int32)
    member = (route_rows[:, None] == expert_range[None, :]).astype(jnp.int32)
    earlier = jnp.cumsum(member, axis=0) - member
    position = jnp.sum(earlier * member, axis=1).astype(jnp.int32)
    active = route_rows % EXP_DEV == 0
    target = jnp.where(active, (route_rows // EXP_DEV) * CAP + position, N_EP * CAP).astype(jnp.int32)
    return active, target


def expert_rows(token_rows, gate_shard, up_shard, down_shard):
    gate_part = jnp.dot(token_rows, gate_shard, preferred_element_type=jnp.float32)
    up_part = jnp.dot(token_rows, up_shard, preferred_element_type=jnp.float32)
    hidden = (jax.nn.silu(gate_part) * up_part).astype(jnp.bfloat16)
    produced = lax.dot_general(hidden, down_shard, (((1,), (1,)), ((), ())), preferred_element_type=jnp.float32)
    return produced.astype(jnp.bfloat16)


def reference(resp_q, resp_kv, prompt_kv, moe_in, routes, gate_probs, w_gate, w_up, w_down):
    queries = resp_q.reshape(GROUPS, RESPONSES, RESP_LEN, KVH, HQ // KVH, HD)
    resp_pairs = resp_kv.reshape(GROUPS, RESPONSES, RESP_LEN, 2, KVH, HD)
    prompts = prompt_kv.reshape(GROUPS, PROMPT, 2, KVH, HD)

    def one_group(members):
        group_q, group_kv, group_prompt = members
        return lax.map(lambda inner: attend_response(inner[0], inner[1], group_prompt), (group_q, group_kv))

    context = lax.map(one_group, (queries, resp_pairs, prompts)).reshape(TOKENS, HQ * HD)

    tokens_grouped = moe_in.reshape(GROUPS, N_EP, TOK_DEV, D)
    routes_grouped = routes.reshape(GROUPS, N_EP, TOK_DEV * TOPK)
    probs_grouped = gate_probs.reshape(GROUPS, N_EP, TOK_DEV * TOPK)

    def group_experts(members):
        token_block, route_block, prob_block = members
        active, target = jax.vmap(slot_layout)(route_block)
        repeated = jnp.repeat(token_block, TOPK, axis=1)

        def place(token_rows, spots):
            return jnp.zeros((N_EP * CAP, D), jnp.bfloat16).at[spots].set(token_rows, mode="drop")

        buffers = jax.vmap(place)(repeated, target).reshape(N_EP, N_EP, CAP, D)
        by_expert = jnp.transpose(buffers, (1, 0, 2, 3)).reshape(N_EP, N_EP * CAP, D)
        outputs = lax.map(lambda inner: expert_rows(*inner), (by_expert, w_gate, w_up, w_down))
        returned = jnp.transpose(outputs.reshape(N_EP, N_EP, CAP, D), (1, 0, 2, 3)).reshape(N_EP, N_EP * CAP, D)
        picked = jax.vmap(lambda table, spots: jnp.take(table, jnp.minimum(spots, N_EP * CAP - 1), axis=0))(returned, target)
        weighting = jnp.where(active, prob_block, 0.0).astype(jnp.float32)
        summed = (picked.astype(jnp.float32) * weighting[..., None]).reshape(N_EP, TOK_DEV, TOPK, D)
        return jnp.sum(summed, axis=2).astype(jnp.bfloat16)

    moe_out = lax.map(group_experts, (tokens_grouped, routes_grouped, probs_grouped)).reshape(TOKENS, D)
    return (context, moe_out)
```

```python
import jax
import jax.numpy as jnp
from jax import lax
from jax.experimental import pallas as pl
from jax.experimental.pallas import tpu as pltpu
from jax.sharding import PartitionSpec as P

D = 2048
FF = 768
HQ = 32
KVH = 2
HD = 128
TOPK = 8
TOK = 128
CAP = 16
EXP_DEV = 4
SHARD = 128
PROMPT_ROWS = 24
NX, NY, NZ = 4, 8, 8
NEP = NX * NZ
SLOTS = NEP * CAP
HALF = SLOTS // 2
MESH = pl.DeviceIdType.MESH
SCALE = HD ** -0.5


def layer_kernel(
    q_hbm, resp_kv, prompt_kv, moe_in, routes_t, gates_t, wg_hbm, wu_hbm, wd_hbm,
    ctx_hbm, moe_out,
    weights, outgoing, received, hidden, produced, returned, gate_hi, gate_lo,
    q_buf, ctx_buf, prompt_buf, keys, values,
    local_sem, ring_send, ring_recv, sib_send, sib_recv, pz_send, pz_recv, px_send, px_recv,
    disp_send, disp_recv, ret_send, ret_recv,
):
    grp = lax.axis_index("grp")
    ep = lax.axis_index("ep")
    y, core = grp // 2, grp % 2
    z, x = ep // NX, ep % NX
    sibling = y * 2 + (1 - core)
    right = ((y + 1) % NY) * 2 + core
    left = ((y + NY - 1) % NY) * 2 + core
    shards = (wg_hbm, wu_hbm, wd_hbm)

    barrier = pltpu.get_barrier_semaphore()
    for other in (sibling, right, left):
        pl.semaphore_signal(barrier, inc=1, device_id=(other, ep), device_id_type=MESH)

    @pl.loop(1, NEP)
    def _(d):
        pl.semaphore_signal(barrier, inc=1, device_id=(grp, (ep + d) % NEP), device_id_type=MESH)

    def own_rows(origin):
        return pl.ds(pl.multiple_of(origin * SHARD, SHARD), SHARD)

    q_copy = pltpu.make_async_copy(q_hbm, q_buf, local_sem.at[0])
    q_copy.start()
    own_copies = [
        pltpu.make_async_copy(shards[m], weights.at[m, own_rows(grp), :], local_sem.at[1 + m])
        for m in range(3)
    ]
    for copy in own_copies:
        copy.start()

    rows = prompt_kv[...].astype(jnp.float32)
    prompt_buf[x, z] = jnp.concatenate(
        [rows[:, : KVH * HD], rows[:, KVH * HD :]], axis=0
    ).astype(jnp.bfloat16)

    owner_expert = lax.broadcasted_iota(jnp.int32, (NEP, TOK), 0) * EXP_DEV
    member = jnp.zeros((NEP, TOK), jnp.float32)
    gate = jnp.zeros((NEP, TOK), jnp.float32)
    for k in range(TOPK):
        hit = routes_t[k : k + 1, :] == owner_expert
        member = member + jnp.where(hit, 1.0, 0.0)
        gate = gate + jnp.where(hit, gates_t[k : k + 1, :], 0.0)
    earlier = lax.broadcasted_iota(jnp.int32, (TOK, TOK), 0) < lax.broadcasted_iota(
        jnp.int32, (TOK, TOK), 1
    )
    position = jnp.dot(
        member.astype(jnp.bfloat16),
        jnp.where(earlier, 1.0, 0.0).astype(jnp.bfloat16),
        preferred_element_type=jnp.float32,
    )
    position = jnp.where(member > 0.0, position, -1.0)
    slot = lax.broadcasted_iota(jnp.int32, (NEP, CAP, TOK), 1).astype(jnp.float32)
    taken = jnp.broadcast_to(position[:, None, :], (NEP, CAP, TOK)) == slot
    onehot = jnp.where(taken, 1.0, 0.0).reshape(SLOTS, TOK).astype(jnp.bfloat16)
    for n in range(D // 256):
        outgoing[:, n * 256 : (n + 1) * 256] = jnp.dot(
            onehot, moe_in[:, n * 256 : (n + 1) * 256], preferred_element_type=jnp.float32
        ).astype(jnp.bfloat16)

    pl.semaphore_wait(barrier, NEP + 2)

    def ring_copy(direction, step, m):
        target = right if direction == 0 else left
        origin = ((y + NY - (step - 1)) % NY if direction == 0 else (y + step - 1) % NY) * 2 + core
        if step == NY // 2:
            start = pl.multiple_of(origin * SHARD + direction * (SHARD // 2), SHARD // 2)
            span = pl.ds(start, SHARD // 2)
        else:
            span = own_rows(origin)
        dst = weights.at[m, span, :]
        src = shards[m] if step == 1 else dst
        return pltpu.make_async_remote_copy(
            src_ref=src, dst_ref=dst,
            send_sem=ring_send.at[direction, step - 1, m],
            recv_sem=ring_recv.at[direction, step - 1, m],
            device_id=(target, ep), device_id_type=MESH,
        )

    def ring_arrival(direction, step, m):
        origin = ((y + NY - step) % NY if direction == 0 else (y + step) % NY) * 2 + core
        if step == NY // 2:
            start = pl.multiple_of(origin * SHARD + direction * (SHARD // 2), SHARD // 2)
            span = pl.ds(start, SHARD // 2)
        else:
            span = own_rows(origin)
        return weights.at[m, span, :]

    def sib_copy(kind, src, dst, m):
        return pltpu.make_async_remote_copy(
            src_ref=src, dst_ref=dst,
            send_sem=sib_send.at[kind, m], recv_sem=sib_recv.at[kind, m],
            device_id=(sibling, ep), device_id_type=MESH,
        )

    def pz_copy(d):
        return pltpu.make_async_remote_copy(
            src_ref=prompt_buf.at[x, z], dst_ref=prompt_buf.at[x, z],
            send_sem=pz_send.at[d - 1], recv_sem=pz_recv.at[d - 1],
            device_id=(grp, ((z + d) % NZ) * NX + x), device_id_type=MESH,
        )

    def px_copy(d):
        return pltpu.make_async_remote_copy(
            src_ref=prompt_buf.at[x], dst_ref=prompt_buf.at[x],
            send_sem=px_send.at[d - 1], recv_sem=px_recv.at[d - 1],
            device_id=(grp, z * NX + (x + d) % NX), device_id_type=MESH,
        )

    def place(source):
        return pl.ds(pl.multiple_of(((source % NX) * NZ + source // NX) * CAP, CAP), CAP)

    def owner_rows(owner):
        return pl.ds(pl.multiple_of(owner * CAP, CAP), CAP)

    def disp_copy(d):
        owner = (ep + d) % NEP
        return pltpu.make_async_remote_copy(
            src_ref=outgoing.at[owner_rows(owner), :], dst_ref=received.at[place(ep), :],
            send_sem=disp_send.at[d], recv_sem=disp_recv.at[d],
            device_id=(grp, owner), device_id_type=MESH,
        )

    def disp_arrival(d):
        source = (ep + NEP - d) % NEP
        return pltpu.make_async_remote_copy(
            src_ref=outgoing.at[owner_rows(source), :], dst_ref=received.at[place(source), :],
            send_sem=disp_send.at[d], recv_sem=disp_recv.at[d],
            device_id=(grp, source), device_id_type=MESH,
        )

    def ret_copy(source):
        d = (source + NEP - ep) % NEP
        return pltpu.make_async_remote_copy(
            src_ref=produced.at[place(source), :], dst_ref=returned.at[owner_rows(ep), :],
            send_sem=ret_send.at[d], recv_sem=ret_recv.at[d],
            device_id=(grp, source), device_id_type=MESH,
        )

    def ret_arrival(d):
        owner = (ep + NEP - d) % NEP
        return pltpu.make_async_remote_copy(
            src_ref=produced.at[place(owner), :], dst_ref=returned.at[owner_rows(owner), :],
            send_sem=ret_send.at[d], recv_sem=ret_recv.at[d],
            device_id=(grp, owner), device_id_type=MESH,
        )

    for d in range(1, NZ):
        pz_copy(d).start()
    for m in range(3):
        for direction in range(2):
            ring_copy(direction, 1, m).start()
    for m in range(3):
        sib_copy(0, shards[m], weights.at[m, own_rows(grp), :], m).start()

    @pl.loop(1, NEP)
    def _(d):
        disp_copy(d).start()

    received[place(ep), :] = outgoing[owner_rows(ep), :]

    spread = jnp.where(taken, jnp.broadcast_to(gate[:, None, :], (NEP, CAP, TOK)), 0.0)
    spread = spread.reshape(SLOTS, TOK).T
    high = spread.astype(jnp.bfloat16)
    gate_hi[...] = high
    gate_lo[...] = (spread - high.astype(jnp.float32)).astype(jnp.bfloat16)

    for d in range(1, NZ):
        pz_copy(d).wait_recv()
    for d in range(1, NX):
        px_copy(d).start()

    def ring_turn(step, m):
        for direction in range(2):
            landed = ring_arrival(direction, step, m)
            pltpu.make_async_remote_copy(
                src_ref=landed, dst_ref=landed,
                send_sem=ring_send.at[direction, step - 1, m],
                recv_sem=ring_recv.at[direction, step - 1, m],
                device_id=(right if direction == 0 else left, ep), device_id_type=MESH,
            ).wait_recv()
            if step < NY // 2:
                ring_copy(direction, step + 1, m).start()
            sib_copy(1 + direction * (NY // 2) + step - 1, landed, landed, m).start()

    def gather_prompt():
        for d in range(1, NX):
            px_copy(d).wait_recv()

        @pl.loop(0, NEP // 2)
        def _(i):
            first = prompt_buf[i // 4, (i % 4) * 2].astype(jnp.float32)
            second = prompt_buf[i // 4, (i % 4) * 2 + 1].astype(jnp.float32)
            at = pl.ds(pl.multiple_of(i * 2 * PROMPT_ROWS, 2 * PROMPT_ROWS), 2 * PROMPT_ROWS)
            keys[at, :] = jnp.concatenate(
                [first[:PROMPT_ROWS], second[:PROMPT_ROWS]], axis=0
            ).astype(jnp.bfloat16)
            values[at, :] = jnp.concatenate(
                [first[PROMPT_ROWS:], second[PROMPT_ROWS:]], axis=0
            ).astype(jnp.bfloat16)

    causal = lax.broadcasted_iota(jnp.int32, (TOK, TOK), 1) <= lax.broadcasted_iota(
        jnp.int32, (TOK, TOK), 0
    )

    def attend(first, last):
        @pl.loop(first, last)
        def _(head):
            at = pl.ds(pl.multiple_of(head * HD, HD), HD)
            kv = pl.ds(pl.multiple_of((head // (HQ // KVH)) * HD, HD), HD)
            kv_value = pl.ds(pl.multiple_of(KVH * HD + (head // (HQ // KVH)) * HD, HD), HD)
            query = q_buf[:, at]
            contract = (((1,), (1,)), ((), ()))
            shared = lax.dot_general(
                query, keys[:, kv], contract, preferred_element_type=jnp.float32
            )
            own = lax.dot_general(
                query, resp_kv[:, kv], contract, preferred_element_type=jnp.float32
            )
            own = jnp.where(causal, own, -jnp.inf)
            top = jnp.maximum(
                jnp.max(shared, axis=-1, keepdims=True), jnp.max(own, axis=-1, keepdims=True)
            )
            shared = jnp.exp((shared - top) * SCALE)
            own = jnp.exp((own - top) * SCALE)
            denominator = jnp.sum(shared, axis=-1, keepdims=True) + jnp.sum(
                own, axis=-1, keepdims=True
            )
            summed = jnp.dot(
                shared.astype(jnp.bfloat16), values[:, kv], preferred_element_type=jnp.float32
            ) + jnp.dot(
                own.astype(jnp.bfloat16), resp_kv[:, kv_value], preferred_element_type=jnp.float32
            )
            ctx_buf[:, at] = (summed / denominator).astype(jnp.bfloat16)

    q_copy.wait()
    ctx_copy = pltpu.make_async_copy(ctx_buf, ctx_hbm, local_sem.at[4])
    ring_turn(1, 0)
    ring_turn(1, 1)
    gather_prompt()
    ring_turn(1, 2)
    attend(0, 4)
    ring_turn(2, 0)
    attend(4, 8)
    ring_turn(2, 1)
    attend(8, 12)
    ring_turn(2, 2)
    attend(12, 16)
    ring_turn(3, 0)
    attend(16, 20)
    ring_turn(3, 1)
    attend(20, 24)
    ring_turn(3, 2)
    attend(24, 28)
    ring_turn(4, 0)
    attend(28, 32)
    ctx_copy.start()
    ring_turn(4, 1)
    ring_turn(4, 2)

    for copy in own_copies:
        copy.wait()
    for m in range(3):
        for kind in range(1 + NY):
            if kind == 0:
                landed = weights.at[m, own_rows(sibling), :]
            else:
                direction, step = (kind - 1) // (NY // 2), (kind - 1) % (NY // 2) + 1
                origin = (
                    (y + NY - step) % NY if direction == 0 else (y + step) % NY
                ) * 2 + (1 - core)
                if step == NY // 2:
                    start = pl.multiple_of(origin * SHARD + direction * (SHARD // 2), SHARD // 2)
                    landed = weights.at[m, pl.ds(start, SHARD // 2), :]
                else:
                    landed = weights.at[m, own_rows(origin), :]
            sib_copy(kind, landed, landed, m).wait_recv()

    @pl.loop(1, NEP)
    def _(d):
        disp_arrival(d).wait_recv()

    for half in range(2):
        span = slice(half * HALF, (half + 1) * HALF)

        @pl.loop(0, FF // 256)
        def _(n):
            at = pl.ds(pl.multiple_of(n * 256, 256), 256)
            gated = jnp.dot(
                received[span, :], weights[0, :, at], preferred_element_type=jnp.float32
            )
            up = jnp.dot(
                received[span, :], weights[1, :, at], preferred_element_type=jnp.float32
            )
            hidden[span, at] = (gated / (1.0 + jnp.exp(-gated)) * up).astype(jnp.bfloat16)

        @pl.loop(0, D // 256)
        def _(n):
            at = pl.ds(pl.multiple_of(n * 256, 256), 256)
            produced[span, at] = lax.dot_general(
                hidden[span, :], weights[2, at, :], (((1,), (1,)), ((), ())),
                preferred_element_type=jnp.float32,
            ).astype(jnp.bfloat16)

        @pl.loop(0, NEP // 2)
        def _(i):
            source = ((z + i) % NZ) * NX + half * 2 + i // NZ

            @pl.when(source != ep)
            def _():
                ret_copy(source).start()

    returned[owner_rows(ep), :] = produced[place(ep), :]

    @pl.loop(1, NEP)
    def _(d):
        ret_arrival(d).wait_recv()

    for n in range(D // 256):
        at = slice(n * 256, (n + 1) * 256)
        moe_out[:, at] = (
            jnp.dot(gate_hi[...], returned[:, at], preferred_element_type=jnp.float32)
            + jnp.dot(gate_lo[...], returned[:, at], preferred_element_type=jnp.float32)
        ).astype(jnp.bfloat16)

    ctx_copy.wait()
    for m in range(3):
        for direction in range(2):
            for step in range(1, NY // 2 + 1):
                ring_copy(direction, step, m).wait_send()
        for kind in range(1 + NY):
            if kind == 0:
                sent = weights.at[m, own_rows(grp), :]
            else:
                sent = ring_arrival((kind - 1) // (NY // 2), (kind - 1) % (NY // 2) + 1, m)
            sib_copy(kind, sent, sent, m).wait_send()
    for d in range(1, NZ):
        pz_copy(d).wait_send()
    for d in range(1, NX):
        px_copy(d).wait_send()

    @pl.loop(1, NEP)
    def _(d):
        disp_copy(d).wait_send()
        ret_arrival(d).wait_send()


def body(resp_q, resp_kv, prompt_kv, moe_in, routes, gate_probs, w_gate, w_up, w_down):
    vmem = pl.BlockSpec(memory_space=pltpu.VMEM)
    anywhere = pl.BlockSpec(memory_space=pl.ANY)
    bf16 = jnp.bfloat16
    dma = pltpu.SemaphoreType.DMA
    return pl.pallas_call(
        layer_kernel,
        out_shape=(
            jax.ShapeDtypeStruct((TOK, HQ * HD), bf16),
            jax.ShapeDtypeStruct((TOK, D), bf16),
        ),
        in_specs=[anywhere] + [vmem] * 5 + [anywhere] * 3,
        out_specs=(anywhere, vmem),
        scratch_shapes=[
            pltpu.VMEM((3, D, FF), bf16),
            pltpu.VMEM((SLOTS, D), bf16),
            pltpu.VMEM((SLOTS, D), bf16),
            pltpu.VMEM((SLOTS, FF), bf16),
            pltpu.VMEM((SLOTS, D), bf16),
            pltpu.VMEM((SLOTS, D), bf16),
            pltpu.VMEM((TOK, SLOTS), bf16),
            pltpu.VMEM((TOK, SLOTS), bf16),
            pltpu.VMEM((TOK, HQ * HD), bf16),
            pltpu.VMEM((TOK, HQ * HD), bf16),
            pltpu.VMEM((NX, NZ, 2 * PROMPT_ROWS, KVH * HD), bf16),
            pltpu.VMEM((NEP * PROMPT_ROWS, KVH * HD), bf16),
            pltpu.VMEM((NEP * PROMPT_ROWS, KVH * HD), bf16),
            dma((5,)),
            dma((2, NY // 2, 3)),
            dma((2, NY // 2, 3)),
            dma((1 + NY, 3)),
            dma((1 + NY, 3)),
            dma((NZ - 1,)),
            dma((NZ - 1,)),
            dma((NX - 1,)),
            dma((NX - 1,)),
            dma((NEP,)),
            dma((NEP,)),
            dma((NEP,)),
            dma((NEP,)),
        ],
        compiler_params=pltpu.CompilerParams(
            collective_id=0, has_side_effects=True, vmem_limit_bytes=48 * 1024 * 1024
        ),
        cost_estimate=pl.CostEstimate(
            flops=7_000_000_000, bytes_accessed=6_000_000, transcendentals=4_000_000
        ),
    )(
        resp_q, resp_kv, prompt_kv, moe_in, routes.T, gate_probs.T,
        w_gate[0], w_up[0], w_down[0],
    )


def solution(mesh):
    placed = P(("grp", "ep"), None)
    weight = P("ep", "grp", None)
    return jax.shard_map(
        body,
        mesh=mesh,
        in_specs=(placed,) * 6 + (weight,) * 3,
        out_specs=(placed, placed),
        check_vma=False,
    )
```

```python
import jax
import jax.numpy as jnp
from jax import lax
from jax.experimental import pallas as pl
from jax.experimental.pallas import tpu as pltpu
from jax.sharding import PartitionSpec as P

D = 2048
FF = 768
HQ = 32
KVH = 2
HD = 128
TOPK = 8
TOK = 128
CAP = 16
EXP_DEV = 4
SHARD = 128
PROMPT_ROWS = 24
NX, NY, NZ = 4, 8, 8
NEP = NX * NZ
SLOTS = NEP * CAP
HALF = SLOTS // 2
MESH = pl.DeviceIdType.MESH
SCALE = HD ** -0.5
VMEM_LIMIT = 62 * 1024 * 1024


OFFSETS = [divmod(d, NX) for i in range(1, NEP // 2) for d in (i, NEP - i)] + [(NZ // 2, 0)]
Z_ORDER = (1, 7, 2, 6, 3, 5, 4, 0)
X_ORDER = (0, 2, 1, 3)
Y_ORDER = (0, 1, 7, 2, 6, 3, 5, 4)
GROUPS = ((0, 5), (5, 8))


def layer_kernel(
    q_hbm, resp_hbm, prompt_hbm, moe_hbm, routes_hbm, gates_hbm, wg_hbm, wu_hbm, wd_hbm,
    ctx_hbm, moe_out,
    weights, outgoing, received, hidden, produced, returned, gate_hi, gate_lo,
    q_buf, ctx_buf, prompt_buf, keys, values, resp_kv, prompt_kv, moe_in, routes_t, gates_t,
    local_sem, ring_send, ring_recv, sib_send, sib_recv, pz_send, pz_recv, px_send, px_recv,
    disp_send, disp_recv, ret_send, ret_recv,
):
    grp = lax.axis_index("grp")
    ep = lax.axis_index("ep")
    y, core = lax.div(grp, 2), lax.rem(grp, 2)
    z, x = lax.div(ep, NX), lax.rem(ep, NX)
    zs = [lax.rem(z + i, NZ) for i in range(NZ)]
    xs = [lax.rem(x + i, NX) for i in range(NX)]
    ys = [lax.rem(y + i, NY) for i in range(NY)]
    sibling = y * 2 + (1 - core)
    right = ys[1] * 2 + core
    left = ys[NY - 1] * 2 + core
    shards = (wg_hbm, wu_hbm, wd_hbm)

    def in_plane(dz, dx):
        return (grp, zs[dz] * NX + xs[dx])

    loads = [
        pltpu.make_async_copy(src, dst, local_sem.at[i])
        for i, (src, dst) in enumerate(
            [
                (routes_hbm, routes_t), (moe_hbm, moe_in), (prompt_hbm, prompt_kv),
                (gates_hbm, gates_t), (q_hbm, q_buf), (resp_hbm, resp_kv),
            ]
            + [(shards[m], weights.at[m, pl.ds(grp * SHARD, SHARD), :]) for m in range(3)]
        )
    ]
    for load in loads[:4]:
        load.start()

    barrier = pltpu.get_barrier_semaphore()
    for other in (sibling, right, left):
        pl.semaphore_signal(barrier, inc=1, device_id=(other, ep), device_id_type=MESH)
    for dz, dx in OFFSETS:
        pl.semaphore_signal(barrier, inc=1, device_id=in_plane(dz, dx), device_id_type=MESH)
    for load in loads[4:]:
        load.start()

    def shard_rows(origin):
        return pl.ds(pl.multiple_of(origin * SHARD, SHARD), SHARD)

    def ring_span(direction, step, m, of_core):
        origin = ys[(-step if direction == 0 else step) % NY] * 2 + of_core
        if step == NY // 2:
            start = pl.multiple_of(origin * SHARD + direction * (SHARD // 2), SHARD // 2)
            return weights.at[m, pl.ds(start, SHARD // 2), :]
        return weights.at[m, shard_rows(origin), :]

    def ring_copy(direction, step, m):
        dst = ring_span(direction, step - 1, m, core)
        if step == NY // 2:
            origin = ys[(1 - step if direction == 0 else step - 1) % NY] * 2 + core
            start = pl.multiple_of(origin * SHARD + direction * (SHARD // 2), SHARD // 2)
            dst = weights.at[m, pl.ds(start, SHARD // 2), :]
        return pltpu.make_async_remote_copy(
            src_ref=shards[m] if step == 1 else dst, dst_ref=dst,
            send_sem=ring_send.at[direction, step - 1, m],
            recv_sem=ring_recv.at[direction, step - 1, m],
            device_id=(right if direction == 0 else left, ep), device_id_type=MESH,
        )

    def ring_arrival(direction, step, m):
        landed = ring_span(direction, step, m, core)
        return pltpu.make_async_remote_copy(
            src_ref=landed, dst_ref=landed,
            send_sem=ring_send.at[direction, step - 1, m],
            recv_sem=ring_recv.at[direction, step - 1, m],
            device_id=(right if direction == 0 else left, ep), device_id_type=MESH,
        )

    def sib_copy(kind, m, of_core):
        if kind == 0:
            span = weights.at[m, shard_rows(y * 2 + of_core), :]
        else:
            span = ring_span((kind - 1) // (NY // 2), (kind - 1) % (NY // 2) + 1, m, of_core)
        return pltpu.make_async_remote_copy(
            src_ref=shards[m] if kind == 0 else span, dst_ref=span,
            send_sem=sib_send.at[kind, m], recv_sem=sib_recv.at[kind, m],
            device_id=(sibling, ep), device_id_type=MESH,
        )

    def pz_copy(d, arrives=False):
        block = prompt_buf.at[x, zs[-d % NZ] if arrives else z]
        return pltpu.make_async_remote_copy(
            src_ref=block, dst_ref=block, send_sem=pz_send.at[d - 1], recv_sem=pz_recv.at[d - 1],
            device_id=in_plane(d, 0), device_id_type=MESH,
        )

    def px_copy(d, arrives=False):
        block = prompt_buf.at[xs[-d % NX] if arrives else x]
        return pltpu.make_async_remote_copy(
            src_ref=block, dst_ref=block, send_sem=px_send.at[d - 1], recv_sem=px_recv.at[d - 1],
            device_id=in_plane(0, d), device_id_type=MESH,
        )

    def slots_of(dz, dx):
        at = (dz * NX + dx) * CAP
        return slice(at, at + CAP)

    def place_of(dz, dx):
        at = (X_ORDER.index(dx) * NZ + dz) * CAP
        return slice(at, at + CAP)

    def disp_copy(dz, dx):
        k = dz * NX + dx
        return pltpu.make_async_remote_copy(
            src_ref=outgoing.at[slots_of(dz, dx), :],
            dst_ref=received.at[place_of(-dz % NZ, -dx % NX), :],
            send_sem=disp_send.at[k], recv_sem=disp_recv.at[k],
            device_id=in_plane(dz, dx), device_id_type=MESH,
        )

    def ret_copy(dz, dx, group):
        k = dz * NX + dx
        columns = slice(256 * GROUPS[group][0], 256 * GROUPS[group][1])
        return pltpu.make_async_remote_copy(
            src_ref=produced.at[place_of(dz, dx), columns],
            dst_ref=returned.at[slots_of(-dz % NZ, -dx % NX), columns],
            send_sem=ret_send.at[group, k], recv_sem=ret_recv.at[group, k],
            device_id=in_plane(dz, dx), device_id_type=MESH,
        )

    row = lax.broadcasted_iota(jnp.int32, (NEP, TOK), 0)
    owner_z, owner_x = (z + row // NX) % NZ, (x + row % NX) % NX
    owner_expert = (owner_z * NX + owner_x) * EXP_DEV
    loads[0].wait()
    member = jnp.zeros((NEP, TOK), jnp.float32)
    for k in range(TOPK):
        member = member + jnp.where(routes_t[k : k + 1, :] == owner_expert, 1.0, 0.0)
    earlier = lax.broadcasted_iota(jnp.int32, (TOK, TOK), 0) < lax.broadcasted_iota(
        jnp.int32, (TOK, TOK), 1
    )
    position = jnp.dot(
        member.astype(jnp.bfloat16),
        jnp.where(earlier, 1.0, 0.0).astype(jnp.bfloat16),
        preferred_element_type=jnp.float32,
    )
    position = jnp.where(member > 0.0, position, -1.0)
    slot = lax.broadcasted_iota(jnp.int32, (NEP, CAP, TOK), 1).astype(jnp.float32)
    taken = jnp.broadcast_to(position[:, None, :], (NEP, CAP, TOK)) == slot
    onehot = jnp.where(taken, 1.0, 0.0).reshape(SLOTS, TOK).astype(jnp.bfloat16)
    loads[1].wait()
    for n in range(D // 256):
        outgoing[:, n * 256 : (n + 1) * 256] = jnp.dot(
            onehot, moe_in[:, n * 256 : (n + 1) * 256], preferred_element_type=jnp.float32
        ).astype(jnp.bfloat16)

    loads[2].wait()
    rows = prompt_kv[...].astype(jnp.float32)
    prompt_buf[x, z] = jnp.concatenate(
        [rows[:, : KVH * HD], rows[:, KVH * HD :]], axis=0
    ).astype(jnp.bfloat16)

    pl.semaphore_wait(barrier, NEP + 2)
    for m in range(2):
        for direction in range(2):
            ring_copy(direction, 1, m).start()
    for d in range(1, NZ):
        pz_copy(d).start()
    for half in range(2):
        for dz, dx in OFFSETS:
            if dx in X_ORDER[half * 2 : half * 2 + 2]:
                disp_copy(dz, dx).start()
    for m in range(3):
        sib_copy(0, m, core).start()

    received[place_of(0, 0), :] = outgoing[slots_of(0, 0), :]

    loads[3].wait()
    gate = jnp.zeros((NEP, TOK), jnp.float32)
    for k in range(TOPK):
        hit = routes_t[k : k + 1, :] == owner_expert
        gate = gate + jnp.where(hit, gates_t[k : k + 1, :], 0.0)
    spread = jnp.where(taken, jnp.broadcast_to(gate[:, None, :], (NEP, CAP, TOK)), 0.0)
    spread = spread.reshape(SLOTS, TOK).T
    high = spread.astype(jnp.bfloat16)
    gate_hi[...] = high
    gate_lo[...] = (spread - high.astype(jnp.float32)).astype(jnp.bfloat16)

    def ring_turn(step, matrices):
        for m in matrices:
            for direction in range(2):
                ring_arrival(direction, step, m).wait_recv()
                if step < NY // 2:
                    ring_copy(direction, step + 1, m).start()
                sib_copy(1 + direction * (NY // 2) + step - 1, m, core).start()

    ring_turn(1, (0, 1))
    for direction in range(2):
        ring_copy(direction, 1, 2).start()
    for d in range(1, NZ):
        pz_copy(d, arrives=True).wait_recv()
    for d in range(1, NX):
        px_copy(d).start()
    ring_turn(2, (0, 1))
    ring_turn(1, (2,))
    ring_turn(3, (0, 1))
    ring_turn(2, (2,))
    ring_turn(4, (0, 1))
    ring_turn(3, (2,))

    def partners(half):
        return [
            (dz, dx)
            for dz in Z_ORDER
            for dx in X_ORDER[half * 2 : half * 2 + 2]
            if (dz, dx) != (0, 0)
        ]

    def up(half):
        span = slice(half * HALF, (half + 1) * HALF)
        for dz, dx in partners(half):
            disp_copy(-dz % NZ, -dx % NX).wait_recv()
        for n in range(FF // 256):
            at = slice(n * 256, (n + 1) * 256)
            gated = jnp.dot(
                received[span, :], weights[0, :, at], preferred_element_type=jnp.float32
            )
            raised = jnp.dot(
                received[span, :], weights[1, :, at], preferred_element_type=jnp.float32
            )
            hidden[span, at] = (gated / (1.0 + jnp.exp(-gated)) * raised).astype(jnp.bfloat16)

    def down(half, group):
        span = slice(half * HALF, (half + 1) * HALF)
        for n in range(*GROUPS[group]):
            rows = pl.ds(pl.multiple_of(ys[Y_ORDER[n]] * 256, 256), 256)
            produced[span, n * 256 : (n + 1) * 256] = lax.dot_general(
                hidden[span, :], weights[2, rows, :], (((1,), (1,)), ((), ())),
                preferred_element_type=jnp.float32,
            ).astype(jnp.bfloat16)
        for dz, dx in partners(half):
            ret_copy(dz, dx, group).start()

    def sib_wait(m, kinds):
        for kind in kinds:
            sib_copy(kind, m, 1 - core).wait_recv()

    for load in loads[6:]:
        load.wait()
    for m in range(2):
        sib_wait(m, range(1 + NY))
    up(0)
    ring_turn(4, (2,))
    sib_wait(2, (0, 1, 2, 5, 6))
    down(0, 0)
    up(1)
    down(1, 0)
    sib_wait(2, (3, 4, 7, 8))
    down(0, 1)
    down(1, 1)

    returned[slots_of(0, 0), :] = produced[place_of(0, 0), :]

    for d in range(1, NX):
        px_copy(d, arrives=True).wait_recv()

    @pl.loop(0, NEP // 2)
    def _(i):
        first = prompt_buf[i // 4, (i % 4) * 2].astype(jnp.float32)
        second = prompt_buf[i // 4, (i % 4) * 2 + 1].astype(jnp.float32)
        at = pl.ds(pl.multiple_of(i * 2 * PROMPT_ROWS, 2 * PROMPT_ROWS), 2 * PROMPT_ROWS)
        keys[at, :] = jnp.concatenate(
            [first[:PROMPT_ROWS], second[:PROMPT_ROWS]], axis=0
        ).astype(jnp.bfloat16)
        values[at, :] = jnp.concatenate(
            [first[PROMPT_ROWS:], second[PROMPT_ROWS:]], axis=0
        ).astype(jnp.bfloat16)

    causal = lax.broadcasted_iota(jnp.int32, (TOK, TOK), 1) <= lax.broadcasted_iota(
        jnp.int32, (TOK, TOK), 0
    )
    loads[4].wait()
    loads[5].wait()

    @pl.loop(0, HQ, unroll=2)
    def _(head):
        at = pl.ds(pl.multiple_of(head * HD, HD), HD)
        kv = pl.ds(pl.multiple_of((head // (HQ // KVH)) * HD, HD), HD)
        kv_value = pl.ds(pl.multiple_of(KVH * HD + (head // (HQ // KVH)) * HD, HD), HD)
        query = q_buf[:, at]
        contract = (((1,), (1,)), ((), ()))
        shared = lax.dot_general(
            query, keys[:, kv], contract, preferred_element_type=jnp.float32
        )
        own = lax.dot_general(
            query, resp_kv[:, kv], contract, preferred_element_type=jnp.float32
        )
        own = jnp.where(causal, own, -jnp.inf)
        top = jnp.maximum(
            jnp.max(shared, axis=-1, keepdims=True), jnp.max(own, axis=-1, keepdims=True)
        )
        shared = jnp.exp((shared - top) * SCALE)
        own = jnp.exp((own - top) * SCALE)
        denominator = jnp.sum(shared, axis=-1, keepdims=True) + jnp.sum(
            own, axis=-1, keepdims=True
        )
        summed = jnp.dot(
            shared.astype(jnp.bfloat16), values[:, kv], preferred_element_type=jnp.float32
        ) + jnp.dot(
            own.astype(jnp.bfloat16), resp_kv[:, kv_value], preferred_element_type=jnp.float32
        )
        ctx_buf[:, at] = (summed / denominator).astype(jnp.bfloat16)

    ctx_copy = pltpu.make_async_copy(ctx_buf, ctx_hbm, local_sem.at[9])
    ctx_copy.start()

    for m in range(3):
        for direction in range(2):
            for step in range(1, NY // 2 + 1):
                ring_copy(direction, step, m).wait_send()
        for kind in range(1 + NY):
            sib_copy(kind, m, core).wait_send()
    for d in range(1, NZ):
        pz_copy(d).wait_send()
    for d in range(1, NX):
        px_copy(d).wait_send()
    for dz, dx in OFFSETS:
        disp_copy(dz, dx).wait_send()

    ctx_copy.wait()
    for group in range(len(GROUPS)):
        for dz, dx in OFFSETS:
            ret_copy(dz, dx, group).wait_send()
        for dz, dx in OFFSETS:
            ret_copy(dz, dx, group).wait_recv()
        for n in range(*GROUPS[group]):
            at = slice(n * 256, (n + 1) * 256)
            columns = pl.ds(pl.multiple_of(ys[Y_ORDER[n]] * 256, 256), 256)
            moe_out[:, columns] = (
                jnp.dot(gate_hi[...], returned[:, at], preferred_element_type=jnp.float32)
                + jnp.dot(gate_lo[...], returned[:, at], preferred_element_type=jnp.float32)
            ).astype(jnp.bfloat16)


def publish_kernel(ctx, moe, ctx_out, moe_out, ctx_buf, moe_buf, in_sem, out_sem):
    pieces = [(ctx, ctx_buf, ctx_out, i, TOK // 4) for i in range(4)]
    pieces += [(moe, moe_buf, moe_out, i, TOK // 2) for i in range(2)]
    incoming, outgoing = [], []
    for n, (src, buf, dst, i, rows) in enumerate(pieces):
        at = slice(i * rows, (i + 1) * rows)
        incoming.append(pltpu.make_async_copy(src.at[at], buf.at[at], in_sem.at[n]))
        outgoing.append(pltpu.make_async_copy(buf.at[at], dst.at[at], out_sem.at[n]))
    for copy in incoming:
        copy.start()
    for copy, following in zip(incoming, outgoing):
        copy.wait()
        following.start()
    for copy in outgoing:
        copy.wait()


def publish(ctx, moe):
    anywhere = pl.BlockSpec(memory_space=pl.ANY)
    return pl.pallas_call(
        publish_kernel,
        out_shape=tuple(jax.ShapeDtypeStruct(a.shape, a.dtype) for a in (ctx, moe)),
        in_specs=[anywhere] * 2,
        out_specs=(anywhere,) * 2,
        scratch_shapes=[
            pltpu.VMEM(ctx.shape, ctx.dtype),
            pltpu.VMEM(moe.shape, moe.dtype),
            pltpu.SemaphoreType.DMA((6,)),
            pltpu.SemaphoreType.DMA((6,)),
        ],
        compiler_params=pltpu.CompilerParams(vmem_limit_bytes=VMEM_LIMIT),
    )(ctx, moe)


def body(resp_q, resp_kv, prompt_kv, moe_in, routes, gate_probs, w_gate, w_up, w_down):
    vmem = pl.BlockSpec(memory_space=pltpu.VMEM)
    anywhere = pl.BlockSpec(memory_space=pl.ANY)
    bf16 = jnp.bfloat16
    dma = pltpu.SemaphoreType.DMA
    results = pl.pallas_call(
        layer_kernel,
        out_shape=(
            jax.ShapeDtypeStruct((TOK, HQ * HD), bf16),
            jax.ShapeDtypeStruct((TOK, D), bf16),
        ),
        in_specs=[anywhere] * 9,
        out_specs=(anywhere, vmem),
        scratch_shapes=[
            pltpu.VMEM((3, D, FF), bf16),
            pltpu.VMEM((SLOTS, D), bf16),
            pltpu.VMEM((SLOTS, D), bf16),
            pltpu.VMEM((SLOTS, FF), bf16),
            pltpu.VMEM((SLOTS, D), bf16),
            pltpu.VMEM((SLOTS, D), bf16),
            pltpu.VMEM((TOK, SLOTS), bf16),
            pltpu.VMEM((TOK, SLOTS), bf16),
            pltpu.VMEM((TOK, HQ * HD), bf16),
            pltpu.VMEM((TOK, HQ * HD), bf16),
            pltpu.VMEM((NX, NZ, 2 * PROMPT_ROWS, KVH * HD), bf16),
            pltpu.VMEM((NEP * PROMPT_ROWS, KVH * HD), bf16),
            pltpu.VMEM((NEP * PROMPT_ROWS, KVH * HD), bf16),
            pltpu.VMEM((TOK, 2 * KVH * HD), bf16),
            pltpu.VMEM((PROMPT_ROWS, 2 * KVH * HD), bf16),
            pltpu.VMEM((TOK, D), bf16),
            pltpu.VMEM((TOPK, TOK), jnp.int32),
            pltpu.VMEM((TOPK, TOK), jnp.float32),
            dma((10,)),
            dma((2, NY // 2, 3)),
            dma((2, NY // 2, 3)),
            dma((1 + NY, 3)),
            dma((1 + NY, 3)),
            dma((NZ - 1,)),
            dma((NZ - 1,)),
            dma((NX - 1,)),
            dma((NX - 1,)),
            dma((NEP,)),
            dma((NEP,)),
            dma((len(GROUPS), NEP)),
            dma((len(GROUPS), NEP)),
        ],
        compiler_params=pltpu.CompilerParams(
            collective_id=0, has_side_effects=True, vmem_limit_bytes=VMEM_LIMIT
        ),
        cost_estimate=pl.CostEstimate(
            flops=7_000_000_000, bytes_accessed=6_000_000, transcendentals=4_000_000
        ),
    )(
        resp_q, resp_kv, prompt_kv, moe_in, routes.T, gate_probs.T,
        w_gate[0], w_up[0], w_down[0],
    )
    return publish(*results)


def solution(mesh):
    placed = P(("grp", "ep"), None)
    weight = P("ep", "grp", None)
    return jax.shard_map(
        body,
        mesh=mesh,
        in_specs=(placed,) * 6 + (weight,) * 3,
        out_specs=(placed, placed),
        check_vma=False,
    )
```

```python
import jax
import jax.numpy as jnp
from jax import lax
from jax.experimental import pallas as pl
from jax.experimental.pallas import tpu as pltpu
from jax.sharding import PartitionSpec as P

D = 2048
FF = 768
HQ = 32
KVH = 2
HD = 128
TOPK = 8
TOK = 128
CAP = 16
EXP_DEV = 4
SHARD = 128
PROMPT_ROWS = 24
NX, NY, NZ = 4, 8, 8
NEP = NX * NZ
SLOTS = NEP * CAP
HALF = SLOTS // 2
MESH = pl.DeviceIdType.MESH
SCALE = HD ** -0.5
VMEM_LIMIT = 62 * 1024 * 1024


OFFSETS = [divmod(d, NX) for i in range(1, NEP // 2) for d in (i, NEP - i)] + [(NZ // 2, 0)]
Z_ORDER = (1, 7, 2, 6, 3, 5, 4, 0)
X_ORDER = (0, 2, 1, 3)
Y_ORDER = (0, 1, 7, 2, 6, 3, 5, 4)
GROUPS = ((0, 5), (5, 8))
LAST_ORDER = (0, 1, 5, 2, 6, 3, 7, 4)


def layer_kernel(
    q_hbm, resp_hbm, prompt_hbm, moe_hbm, routes_hbm, gates_hbm, wg_hbm, wu_hbm, wd_hbm,
    ctx_hbm, moe_out,
    weights, outgoing, received, hidden, produced, returned, gate_hi, gate_lo,
    q_buf, ctx_buf, prompt_buf, keys, values, resp_kv, prompt_kv, moe_in, routes_t, gates_t,
    local_sem, ring_send, ring_recv, sib_send, sib_recv, pz_send, pz_recv, px_send, px_recv,
    disp_send, disp_recv, ret_send, ret_recv,
):
    grp = lax.axis_index("grp")
    ep = lax.axis_index("ep")
    y, core = lax.div(grp, 2), lax.rem(grp, 2)
    z, x = lax.div(ep, NX), lax.rem(ep, NX)
    zs = [lax.rem(z + i, NZ) for i in range(NZ)]
    xs = [lax.rem(x + i, NX) for i in range(NX)]
    ys = [lax.rem(y + i, NY) for i in range(NY)]
    sibling = y * 2 + (1 - core)
    right = ys[1] * 2 + core
    left = ys[NY - 1] * 2 + core
    shards = (wg_hbm, wu_hbm, wd_hbm)

    def in_plane(dz, dx):
        return (grp, zs[dz] * NX + xs[dx])

    barrier = pltpu.get_barrier_semaphore()
    for dz, dx in reversed(OFFSETS):
        pl.semaphore_signal(barrier, inc=1, device_id=in_plane(dz, dx), device_id_type=MESH)
    for other in (sibling, right, left):
        pl.semaphore_signal(barrier, inc=1, device_id=(other, ep), device_id_type=MESH)

    loads = [
        pltpu.make_async_copy(src, dst, local_sem.at[i])
        for i, (src, dst) in enumerate(
            [
                (routes_hbm, routes_t), (moe_hbm, moe_in), (prompt_hbm, prompt_kv),
                (gates_hbm, gates_t), (q_hbm, q_buf), (resp_hbm, resp_kv),
            ]
            + [(shards[m], weights.at[m, pl.ds(grp * SHARD, SHARD), :]) for m in range(3)]
        )
    ]
    for load in loads[:4]:
        load.start()

    for load in loads[4:]:
        load.start()

    def shard_rows(origin):
        return pl.ds(pl.multiple_of(origin * SHARD, SHARD), SHARD)

    def ring_span(direction, step, m, of_core):
        origin = ys[(-step if direction == 0 else step) % NY] * 2 + of_core
        if step == NY // 2:
            start = pl.multiple_of(origin * SHARD + direction * (SHARD // 2), SHARD // 2)
            return weights.at[m, pl.ds(start, SHARD // 2), :]
        return weights.at[m, shard_rows(origin), :]

    def ring_copy(direction, step, m):
        dst = ring_span(direction, step - 1, m, core)
        if step == NY // 2:
            origin = ys[(1 - step if direction == 0 else step - 1) % NY] * 2 + core
            start = pl.multiple_of(origin * SHARD + direction * (SHARD // 2), SHARD // 2)
            dst = weights.at[m, pl.ds(start, SHARD // 2), :]
        return pltpu.make_async_remote_copy(
            src_ref=shards[m] if step == 1 else dst, dst_ref=dst,
            send_sem=ring_send.at[direction, step - 1, m],
            recv_sem=ring_recv.at[direction, step - 1, m],
            device_id=(right if direction == 0 else left, ep), device_id_type=MESH,
        )

    def ring_arrival(direction, step, m):
        landed = ring_span(direction, step, m, core)
        return pltpu.make_async_remote_copy(
            src_ref=landed, dst_ref=landed,
            send_sem=ring_send.at[direction, step - 1, m],
            recv_sem=ring_recv.at[direction, step - 1, m],
            device_id=(right if direction == 0 else left, ep), device_id_type=MESH,
        )

    def sib_copy(kind, m, of_core):
        if kind == 0:
            span = weights.at[m, shard_rows(y * 2 + of_core), :]
        else:
            span = ring_span((kind - 1) // (NY // 2), (kind - 1) % (NY // 2) + 1, m, of_core)
        return pltpu.make_async_remote_copy(
            src_ref=shards[m] if kind == 0 else span, dst_ref=span,
            send_sem=sib_send.at[kind, m], recv_sem=sib_recv.at[kind, m],
            device_id=(sibling, ep), device_id_type=MESH,
        )

    def pz_copy(d, arrives=False):
        block = prompt_buf.at[x, zs[-d % NZ] if arrives else z]
        return pltpu.make_async_remote_copy(
            src_ref=block, dst_ref=block, send_sem=pz_send.at[d - 1], recv_sem=pz_recv.at[d - 1],
            device_id=in_plane(d, 0), device_id_type=MESH,
        )

    def px_copy(d, arrives=False):
        block = prompt_buf.at[xs[-d % NX] if arrives else x]
        return pltpu.make_async_remote_copy(
            src_ref=block, dst_ref=block, send_sem=px_send.at[d - 1], recv_sem=px_recv.at[d - 1],
            device_id=in_plane(0, d), device_id_type=MESH,
        )

    def slots_of(dz, dx):
        at = (dz * NX + dx) * CAP
        return slice(at, at + CAP)

    def place_of(dz, dx):
        at = (X_ORDER.index(dx) * NZ + dz) * CAP
        return slice(at, at + CAP)

    def disp_copy(dz, dx):
        k = dz * NX + dx
        return pltpu.make_async_remote_copy(
            src_ref=outgoing.at[slots_of(dz, dx), :],
            dst_ref=received.at[place_of(-dz % NZ, -dx % NX), :],
            send_sem=disp_send.at[k], recv_sem=disp_recv.at[k],
            device_id=in_plane(dz, dx), device_id_type=MESH,
        )

    def ret_copy(dz, dx, group):
        k = dz * NX + dx
        columns = slice(256 * GROUPS[group][0], 256 * GROUPS[group][1])
        return pltpu.make_async_remote_copy(
            src_ref=produced.at[place_of(dz, dx), columns],
            dst_ref=returned.at[slots_of(-dz % NZ, -dx % NX), columns],
            send_sem=ret_send.at[group, k], recv_sem=ret_recv.at[group, k],
            device_id=in_plane(dz, dx), device_id_type=MESH,
        )

    row = lax.broadcasted_iota(jnp.int32, (NEP, TOK), 0)
    owner_z, owner_x = (z + row // NX) % NZ, (x + row % NX) % NX
    owner_expert = (owner_z * NX + owner_x) * EXP_DEV
    loads[0].wait()
    member = jnp.zeros((NEP, TOK), jnp.float32)
    for k in range(TOPK):
        member = member + jnp.where(routes_t[k : k + 1, :] == owner_expert, 1.0, 0.0)
    earlier = lax.broadcasted_iota(jnp.int32, (TOK, TOK), 0) < lax.broadcasted_iota(
        jnp.int32, (TOK, TOK), 1
    )
    position = jnp.dot(
        member.astype(jnp.bfloat16),
        jnp.where(earlier, 1.0, 0.0).astype(jnp.bfloat16),
        preferred_element_type=jnp.float32,
    )
    position = jnp.where(member > 0.0, position, -1.0)
    slot = lax.broadcasted_iota(jnp.int32, (NEP, CAP, TOK), 1).astype(jnp.float32)
    taken = jnp.broadcast_to(position[:, None, :], (NEP, CAP, TOK)) == slot
    onehot = jnp.where(taken, 1.0, 0.0).reshape(SLOTS, TOK).astype(jnp.bfloat16)
    loads[1].wait()
    for n in range(D // 256):
        outgoing[:, n * 256 : (n + 1) * 256] = jnp.dot(
            onehot, moe_in[:, n * 256 : (n + 1) * 256], preferred_element_type=jnp.float32
        ).astype(jnp.bfloat16)

    loads[2].wait()
    rows = prompt_kv[...].astype(jnp.float32)
    prompt_buf[x, z] = jnp.concatenate(
        [rows[:, : KVH * HD], rows[:, KVH * HD :]], axis=0
    ).astype(jnp.bfloat16)

    pl.semaphore_wait(barrier, NEP + 2)
    for m in range(2):
        for direction in range(2):
            ring_copy(direction, 1, m).start()
    for half in range(2):
        for dz, dx in OFFSETS:
            if dx in X_ORDER[half * 2 : half * 2 + 2]:
                disp_copy(dz, dx).start()
    for d in range(1, NZ):
        pz_copy(d).start()
    for m in range(3):
        sib_copy(0, m, core).start()

    received[place_of(0, 0), :] = outgoing[slots_of(0, 0), :]

    loads[3].wait()
    gate = jnp.zeros((NEP, TOK), jnp.float32)
    for k in range(TOPK):
        hit = routes_t[k : k + 1, :] == owner_expert
        gate = gate + jnp.where(hit, gates_t[k : k + 1, :], 0.0)
    spread = jnp.where(taken, jnp.broadcast_to(gate[:, None, :], (NEP, CAP, TOK)), 0.0)
    spread = spread.reshape(SLOTS, TOK).T
    high = spread.astype(jnp.bfloat16)
    gate_hi[...] = high
    gate_lo[...] = (spread - high.astype(jnp.float32)).astype(jnp.bfloat16)

    def ring_turn(step, matrices):
        for m in matrices:
            for direction in range(2):
                ring_arrival(direction, step, m).wait_recv()
                if step < NY // 2:
                    ring_copy(direction, step + 1, m).start()
                sib_copy(1 + direction * (NY // 2) + step - 1, m, core).start()

    ring_turn(1, (0, 1))
    for direction in range(2):
        ring_copy(direction, 1, 2).start()
    ring_turn(2, (0, 1))
    ring_turn(1, (2,))
    ring_turn(3, (0, 1))
    ring_turn(2, (2,))
    ring_turn(4, (0, 1))
    ring_turn(3, (2,))

    def partners(half):
        return [
            (dz, dx)
            for dz in Z_ORDER
            for dx in X_ORDER[half * 2 : half * 2 + 2]
            if (dz, dx) != (0, 0)
        ]

    def up(half):
        span = slice(half * HALF, (half + 1) * HALF)
        for dz, dx in partners(half):
            disp_copy(-dz % NZ, -dx % NX).wait_recv()
        for n in range(FF // 256):
            at = slice(n * 256, (n + 1) * 256)
            gated = jnp.dot(
                received[span, :], weights[0, :, at], preferred_element_type=jnp.float32
            )
            raised = jnp.dot(
                received[span, :], weights[1, :, at], preferred_element_type=jnp.float32
            )
            hidden[span, at] = (gated / (1.0 + jnp.exp(-gated)) * raised).astype(jnp.bfloat16)

    def down(half, group):
        span = slice(half * HALF, (half + 1) * HALF)
        for n in range(*GROUPS[group]):
            rows = pl.ds(pl.multiple_of(ys[Y_ORDER[n]] * 256, 256), 256)
            produced[span, n * 256 : (n + 1) * 256] = lax.dot_general(
                hidden[span, :], weights[2, rows, :], (((1,), (1,)), ((), ())),
                preferred_element_type=jnp.float32,
            ).astype(jnp.bfloat16)

    def give_back(half, group):
        for dz, dx in partners(half):
            ret_copy(dz, dx, group).start()

    def give_back_by_z(group):
        for target in LAST_ORDER:
            dz = lax.rem(target - z + NZ, NZ)
            for dx in X_ORDER:
                copy = pltpu.make_async_remote_copy(
                    src_ref=produced.at[
                        pl.ds(pl.multiple_of((X_ORDER.index(dx) * NZ + dz) * CAP, CAP), CAP),
                        slice(256 * GROUPS[group][0], 256 * GROUPS[group][1]),
                    ],
                    dst_ref=returned.at[
                        pl.ds(
                            pl.multiple_of(
                                (lax.rem(NZ - dz, NZ) * NX + (-dx % NX)) * CAP, CAP
                            ),
                            CAP,
                        ),
                        slice(256 * GROUPS[group][0], 256 * GROUPS[group][1]),
                    ],
                    send_sem=ret_send.at[group, dz * NX + dx],
                    recv_sem=ret_recv.at[group, dz * NX + dx],
                    device_id=(grp, target * NX + xs[dx]), device_id_type=MESH,
                )
                if dx == 0:
                    pl.when(target != z)(copy.start)
                else:
                    copy.start()

    def sib_wait(m, kinds):
        for kind in kinds:
            sib_copy(kind, m, 1 - core).wait_recv()

    for load in loads[6:]:
        load.wait()
    for m in range(2):
        sib_wait(m, range(1 + NY))
    up(0)
    ring_turn(4, (2,))
    sib_wait(2, (0, 1, 2, 5, 6))
    down(0, 0)
    give_back(0, 0)
    up(1)
    down(1, 0)
    give_back(1, 0)
    sib_wait(2, (3, 4, 7, 8))
    down(0, 1)
    down(1, 1)
    give_back_by_z(1)

    returned[slots_of(0, 0), :] = produced[place_of(0, 0), :]

    for d in range(1, NZ):
        pz_copy(d, arrives=True).wait_recv()
    for d in range(1, NX):
        px_copy(d).start()
    for d in range(1, NX):
        px_copy(d, arrives=True).wait_recv()

    @pl.loop(0, NEP // 2)
    def _(i):
        first = prompt_buf[i // 4, (i % 4) * 2].astype(jnp.float32)
        second = prompt_buf[i // 4, (i % 4) * 2 + 1].astype(jnp.float32)
        at = pl.ds(pl.multiple_of(i * 2 * PROMPT_ROWS, 2 * PROMPT_ROWS), 2 * PROMPT_ROWS)
        keys[at, :] = jnp.concatenate(
            [first[:PROMPT_ROWS], second[:PROMPT_ROWS]], axis=0
        ).astype(jnp.bfloat16)
        values[at, :] = jnp.concatenate(
            [first[PROMPT_ROWS:], second[PROMPT_ROWS:]], axis=0
        ).astype(jnp.bfloat16)

    causal = lax.broadcasted_iota(jnp.int32, (TOK, TOK), 1) <= lax.broadcasted_iota(
        jnp.int32, (TOK, TOK), 0
    )
    loads[4].wait()
    loads[5].wait()

    @pl.loop(0, HQ, unroll=2)
    def _(head):
        at = pl.ds(pl.multiple_of(head * HD, HD), HD)
        kv = pl.ds(pl.multiple_of((head // (HQ // KVH)) * HD, HD), HD)
        kv_value = pl.ds(pl.multiple_of(KVH * HD + (head // (HQ // KVH)) * HD, HD), HD)
        query = q_buf[:, at]
        contract = (((1,), (1,)), ((), ()))
        shared = lax.dot_general(
            query, keys[:, kv], contract, preferred_element_type=jnp.float32
        )
        own = lax.dot_general(
            query, resp_kv[:, kv], contract, preferred_element_type=jnp.float32
        )
        own = jnp.where(causal, own, -jnp.inf)
        top = jnp.maximum(
            jnp.max(shared, axis=-1, keepdims=True), jnp.max(own, axis=-1, keepdims=True)
        )
        shared = jnp.exp((shared - top) * SCALE)
        own = jnp.exp((own - top) * SCALE)
        denominator = jnp.sum(shared, axis=-1, keepdims=True) + jnp.sum(
            own, axis=-1, keepdims=True
        )
        summed = jnp.dot(
            shared.astype(jnp.bfloat16), values[:, kv], preferred_element_type=jnp.float32
        ) + jnp.dot(
            own.astype(jnp.bfloat16), resp_kv[:, kv_value], preferred_element_type=jnp.float32
        )
        ctx_buf[:, at] = (summed / denominator).astype(jnp.bfloat16)

    ctx_copy = pltpu.make_async_copy(ctx_buf, ctx_hbm, local_sem.at[9])
    ctx_copy.start()

    for m in range(3):
        for direction in range(2):
            for step in range(1, NY // 2 + 1):
                ring_copy(direction, step, m).wait_send()
        for kind in range(1 + NY):
            sib_copy(kind, m, core).wait_send()
    for d in range(1, NZ):
        pz_copy(d).wait_send()
    for d in range(1, NX):
        px_copy(d).wait_send()
    for dz, dx in OFFSETS:
        disp_copy(dz, dx).wait_send()

    ctx_copy.wait()
    for group in range(len(GROUPS)):
        for dz, dx in OFFSETS:
            ret_copy(dz, dx, group).wait_send()
        for dz, dx in OFFSETS:
            ret_copy(dz, dx, group).wait_recv()
        for n in range(*GROUPS[group]):
            at = slice(n * 256, (n + 1) * 256)
            columns = pl.ds(pl.multiple_of(ys[Y_ORDER[n]] * 256, 256), 256)
            moe_out[:, columns] = (
                jnp.dot(gate_hi[...], returned[:, at], preferred_element_type=jnp.float32)
                + jnp.dot(gate_lo[...], returned[:, at], preferred_element_type=jnp.float32)
            ).astype(jnp.bfloat16)


def publish_kernel(ctx, moe, ctx_out, moe_out, ctx_buf, moe_buf, in_sem, out_sem):
    pieces = [(ctx, ctx_buf, ctx_out, i, TOK // 4) for i in range(4)]
    pieces += [(moe, moe_buf, moe_out, i, TOK // 2) for i in range(2)]
    incoming, outgoing = [], []
    for n, (src, buf, dst, i, rows) in enumerate(pieces):
        at = slice(i * rows, (i + 1) * rows)
        incoming.append(pltpu.make_async_copy(src.at[at], buf.at[at], in_sem.at[n]))
        outgoing.append(pltpu.make_async_copy(buf.at[at], dst.at[at], out_sem.at[n]))
    for copy in incoming:
        copy.start()
    for copy, following in zip(incoming, outgoing):
        copy.wait()
        following.start()
    for copy in outgoing:
        copy.wait()


def publish(ctx, moe):
    anywhere = pl.BlockSpec(memory_space=pl.ANY)
    return pl.pallas_call(
        publish_kernel,
        out_shape=tuple(jax.ShapeDtypeStruct(a.shape, a.dtype) for a in (ctx, moe)),
        in_specs=[anywhere] * 2,
        out_specs=(anywhere,) * 2,
        scratch_shapes=[
            pltpu.VMEM(ctx.shape, ctx.dtype),
            pltpu.VMEM(moe.shape, moe.dtype),
            pltpu.SemaphoreType.DMA((6,)),
            pltpu.SemaphoreType.DMA((6,)),
        ],
        compiler_params=pltpu.CompilerParams(vmem_limit_bytes=VMEM_LIMIT),
    )(ctx, moe)


def body(resp_q, resp_kv, prompt_kv, moe_in, routes, gate_probs, w_gate, w_up, w_down):
    vmem = pl.BlockSpec(memory_space=pltpu.VMEM)
    anywhere = pl.BlockSpec(memory_space=pl.ANY)
    bf16 = jnp.bfloat16
    dma = pltpu.SemaphoreType.DMA
    results = pl.pallas_call(
        layer_kernel,
        out_shape=(
            jax.ShapeDtypeStruct((TOK, HQ * HD), bf16),
            jax.ShapeDtypeStruct((TOK, D), bf16),
        ),
        in_specs=[anywhere] * 9,
        out_specs=(anywhere, vmem),
        scratch_shapes=[
            pltpu.VMEM((3, D, FF), bf16),
            pltpu.VMEM((SLOTS, D), bf16),
            pltpu.VMEM((SLOTS, D), bf16),
            pltpu.VMEM((SLOTS, FF), bf16),
            pltpu.VMEM((SLOTS, D), bf16),
            pltpu.VMEM((SLOTS, D), bf16),
            pltpu.VMEM((TOK, SLOTS), bf16),
            pltpu.VMEM((TOK, SLOTS), bf16),
            pltpu.VMEM((TOK, HQ * HD), bf16),
            pltpu.VMEM((TOK, HQ * HD), bf16),
            pltpu.VMEM((NX, NZ, 2 * PROMPT_ROWS, KVH * HD), bf16),
            pltpu.VMEM((NEP * PROMPT_ROWS, KVH * HD), bf16),
            pltpu.VMEM((NEP * PROMPT_ROWS, KVH * HD), bf16),
            pltpu.VMEM((TOK, 2 * KVH * HD), bf16),
            pltpu.VMEM((PROMPT_ROWS, 2 * KVH * HD), bf16),
            pltpu.VMEM((TOK, D), bf16),
            pltpu.VMEM((TOPK, TOK), jnp.int32),
            pltpu.VMEM((TOPK, TOK), jnp.float32),
            dma((10,)),
            dma((2, NY // 2, 3)),
            dma((2, NY // 2, 3)),
            dma((1 + NY, 3)),
            dma((1 + NY, 3)),
            dma((NZ - 1,)),
            dma((NZ - 1,)),
            dma((NX - 1,)),
            dma((NX - 1,)),
            dma((NEP,)),
            dma((NEP,)),
            dma((len(GROUPS), NEP)),
            dma((len(GROUPS), NEP)),
        ],
        compiler_params=pltpu.CompilerParams(
            collective_id=0, has_side_effects=True, vmem_limit_bytes=VMEM_LIMIT
        ),
        cost_estimate=pl.CostEstimate(
            flops=7_000_000_000, bytes_accessed=6_000_000, transcendentals=4_000_000
        ),
    )(
        resp_q, resp_kv, prompt_kv, moe_in, routes.T, gate_probs.T,
        w_gate[0], w_up[0], w_down[0],
    )
    return publish(*results)


def solution(mesh):
    placed = P(("grp", "ep"), None)
    weight = P("ep", "grp", None)
    return jax.shard_map(
        body,
        mesh=mesh,
        in_specs=(placed,) * 6 + (weight,) * 3,
        out_specs=(placed, placed),
        check_vma=False,
    )
```

```python
import jax
import jax.numpy as jnp
from jax import lax
from jax.experimental import pallas as pl
from jax.experimental.pallas import tpu as pltpu
from jax.sharding import PartitionSpec as P

D = 2048
FF = 768
HQ = 32
KVH = 2
HD = 128
TOPK = 8
TOK = 128
CAP = 16
EXP_DEV = 4
SHARD = 128
PROMPT_ROWS = 24
NX, NY, NZ = 4, 8, 8
NEP = NX * NZ
SLOTS = NEP * CAP
HALF = SLOTS // 2
MESH = pl.DeviceIdType.MESH
SCALE = HD ** -0.5
VMEM_LIMIT = 62 * 1024 * 1024


OFFSETS = [divmod(d, NX) for i in range(1, NEP // 2) for d in (i, NEP - i)] + [(NZ // 2, 0)]
Z_ORDER = (1, 7, 2, 6, 3, 5, 4, 0)
X_ORDER = (0, 2, 1, 3)
Y_ORDER = (0, 1, 7, 2, 6, 3, 5, 4)
GROUPS = ((0, 5), (5, 8))
LAST_ORDER = (0, 1, 5, 2, 6, 3, 7, 4)


def layer_kernel(
    q_hbm, resp_hbm, prompt_hbm, moe_hbm, routes_hbm, gates_hbm, wg_hbm, wu_hbm, wd_hbm,
    ctx_hbm, moe_hbm_out,
    weights, outgoing, received, hidden, produced, returned, gate_hi, gate_lo,
    q_buf, ctx_buf, prompt_buf, keys, values, resp_kv, prompt_kv, moe_in, routes_t, gates_t, moe_out,
    local_sem, ring_send, ring_recv, sib_send, sib_recv, pz_send, pz_recv, px_send, px_recv,
    disp_send, disp_recv, ret_send, ret_recv,
):
    grp = lax.axis_index("grp")
    ep = lax.axis_index("ep")
    y, core = lax.div(grp, 2), lax.rem(grp, 2)
    z, x = lax.div(ep, NX), lax.rem(ep, NX)
    zs = [lax.rem(z + i, NZ) for i in range(NZ)]
    xs = [lax.rem(x + i, NX) for i in range(NX)]
    ys = [lax.rem(y + i, NY) for i in range(NY)]
    sibling = y * 2 + (1 - core)
    right = ys[1] * 2 + core
    left = ys[NY - 1] * 2 + core
    shards = (wg_hbm, wu_hbm, wd_hbm)

    def in_plane(dz, dx):
        return (grp, zs[dz] * NX + xs[dx])

    barrier = pltpu.get_barrier_semaphore()
    for dz, dx in reversed(OFFSETS):
        pl.semaphore_signal(barrier, inc=1, device_id=in_plane(dz, dx), device_id_type=MESH)
    for other in (sibling, right, left):
        pl.semaphore_signal(barrier, inc=1, device_id=(other, ep), device_id_type=MESH)

    loads = [
        pltpu.make_async_copy(src, dst, local_sem.at[i])
        for i, (src, dst) in enumerate(
            [
                (routes_hbm, routes_t), (moe_hbm, moe_in), (prompt_hbm, prompt_kv),
                (gates_hbm, gates_t), (q_hbm, q_buf), (resp_hbm, resp_kv),
            ]
            + [(shards[m], weights.at[m, pl.ds(grp * SHARD, SHARD), :]) for m in range(3)]
        )
    ]
    for load in loads[:4]:
        load.start()

    for load in loads[4:]:
        load.start()

    def shard_rows(origin):
        return pl.ds(pl.multiple_of(origin * SHARD, SHARD), SHARD)

    def ring_span(direction, step, m, of_core):
        origin = ys[(-step if direction == 0 else step) % NY] * 2 + of_core
        if step == NY // 2:
            start = pl.multiple_of(origin * SHARD + direction * (SHARD // 2), SHARD // 2)
            return weights.at[m, pl.ds(start, SHARD // 2), :]
        return weights.at[m, shard_rows(origin), :]

    def ring_copy(direction, step, m):
        dst = ring_span(direction, step - 1, m, core)
        if step == NY // 2:
            origin = ys[(1 - step if direction == 0 else step - 1) % NY] * 2 + core
            start = pl.multiple_of(origin * SHARD + direction * (SHARD // 2), SHARD // 2)
            dst = weights.at[m, pl.ds(start, SHARD // 2), :]
        return pltpu.make_async_remote_copy(
            src_ref=shards[m] if step == 1 else dst, dst_ref=dst,
            send_sem=ring_send.at[direction, step - 1, m],
            recv_sem=ring_recv.at[direction, step - 1, m],
            device_id=(right if direction == 0 else left, ep), device_id_type=MESH,
        )

    def ring_arrival(direction, step, m):
        landed = ring_span(direction, step, m, core)
        return pltpu.make_async_remote_copy(
            src_ref=landed, dst_ref=landed,
            send_sem=ring_send.at[direction, step - 1, m],
            recv_sem=ring_recv.at[direction, step - 1, m],
            device_id=(right if direction == 0 else left, ep), device_id_type=MESH,
        )

    def sib_copy(kind, m, of_core):
        if kind == 0:
            span = weights.at[m, shard_rows(y * 2 + of_core), :]
        else:
            span = ring_span((kind - 1) // (NY // 2), (kind - 1) % (NY // 2) + 1, m, of_core)
        return pltpu.make_async_remote_copy(
            src_ref=shards[m] if kind == 0 else span, dst_ref=span,
            send_sem=sib_send.at[kind, m], recv_sem=sib_recv.at[kind, m],
            device_id=(sibling, ep), device_id_type=MESH,
        )

    def pz_copy(d, arrives=False):
        block = prompt_buf.at[x, zs[-d % NZ] if arrives else z]
        return pltpu.make_async_remote_copy(
            src_ref=block, dst_ref=block, send_sem=pz_send.at[d - 1], recv_sem=pz_recv.at[d - 1],
            device_id=in_plane(d, 0), device_id_type=MESH,
        )

    def px_copy(d, arrives=False):
        block = prompt_buf.at[xs[-d % NX] if arrives else x]
        return pltpu.make_async_remote_copy(
            src_ref=block, dst_ref=block, send_sem=px_send.at[d - 1], recv_sem=px_recv.at[d - 1],
            device_id=in_plane(0, d), device_id_type=MESH,
        )

    def slots_of(dz, dx):
        at = (dz * NX + dx) * CAP
        return slice(at, at + CAP)

    def place_of(dz, dx):
        at = (X_ORDER.index(dx) * NZ + dz) * CAP
        return slice(at, at + CAP)

    def disp_copy(dz, dx):
        k = dz * NX + dx
        return pltpu.make_async_remote_copy(
            src_ref=outgoing.at[slots_of(dz, dx), :],
            dst_ref=received.at[place_of(-dz % NZ, -dx % NX), :],
            send_sem=disp_send.at[k], recv_sem=disp_recv.at[k],
            device_id=in_plane(dz, dx), device_id_type=MESH,
        )

    def ret_copy(dz, dx, group):
        k = dz * NX + dx
        columns = slice(256 * GROUPS[group][0], 256 * GROUPS[group][1])
        return pltpu.make_async_remote_copy(
            src_ref=produced.at[place_of(dz, dx), columns],
            dst_ref=returned.at[slots_of(-dz % NZ, -dx % NX), columns],
            send_sem=ret_send.at[group, k], recv_sem=ret_recv.at[group, k],
            device_id=in_plane(dz, dx), device_id_type=MESH,
        )

    row = lax.broadcasted_iota(jnp.int32, (NEP, TOK), 0)
    owner_z, owner_x = (z + row // NX) % NZ, (x + row % NX) % NX
    owner_expert = (owner_z * NX + owner_x) * EXP_DEV
    loads[0].wait()
    member = jnp.zeros((NEP, TOK), jnp.float32)
    for k in range(TOPK):
        member = member + jnp.where(routes_t[k : k + 1, :] == owner_expert, 1.0, 0.0)
    earlier = lax.broadcasted_iota(jnp.int32, (TOK, TOK), 0) < lax.broadcasted_iota(
        jnp.int32, (TOK, TOK), 1
    )
    position = jnp.dot(
        member.astype(jnp.bfloat16),
        jnp.where(earlier, 1.0, 0.0).astype(jnp.bfloat16),
        preferred_element_type=jnp.float32,
    )
    position = jnp.where(member > 0.0, position, -1.0)
    slot = lax.broadcasted_iota(jnp.int32, (NEP, CAP, TOK), 1).astype(jnp.float32)
    taken = jnp.broadcast_to(position[:, None, :], (NEP, CAP, TOK)) == slot
    onehot = jnp.where(taken, 1.0, 0.0).reshape(SLOTS, TOK).astype(jnp.bfloat16)
    loads[1].wait()
    for n in range(D // 256):
        outgoing[:, n * 256 : (n + 1) * 256] = jnp.dot(
            onehot, moe_in[:, n * 256 : (n + 1) * 256], preferred_element_type=jnp.float32
        ).astype(jnp.bfloat16)

    loads[2].wait()
    rows = prompt_kv[...].astype(jnp.float32)
    prompt_buf[x, z] = jnp.concatenate(
        [rows[:, : KVH * HD], rows[:, KVH * HD :]], axis=0
    ).astype(jnp.bfloat16)

    pl.semaphore_wait(barrier, NEP + 2)
    for m in range(2):
        for direction in range(2):
            ring_copy(direction, 1, m).start()
    for half in range(2):
        for dz, dx in OFFSETS:
            if dx in X_ORDER[half * 2 : half * 2 + 2]:
                disp_copy(dz, dx).start()
    for d in range(1, NZ):
        pz_copy(d).start()
    for m in range(3):
        sib_copy(0, m, core).start()

    received[place_of(0, 0), :] = outgoing[slots_of(0, 0), :]

    loads[3].wait()
    gate = jnp.zeros((NEP, TOK), jnp.float32)
    for k in range(TOPK):
        hit = routes_t[k : k + 1, :] == owner_expert
        gate = gate + jnp.where(hit, gates_t[k : k + 1, :], 0.0)
    spread = jnp.where(taken, jnp.broadcast_to(gate[:, None, :], (NEP, CAP, TOK)), 0.0)
    spread = spread.reshape(SLOTS, TOK).T
    high = spread.astype(jnp.bfloat16)
    gate_hi[...] = high
    gate_lo[...] = (spread - high.astype(jnp.float32)).astype(jnp.bfloat16)

    def ring_turn(step, matrices):
        for m in matrices:
            for direction in range(2):
                ring_arrival(direction, step, m).wait_recv()
                if step < NY // 2:
                    ring_copy(direction, step + 1, m).start()
                sib_copy(1 + direction * (NY // 2) + step - 1, m, core).start()

    ring_turn(1, (0, 1))
    for direction in range(2):
        ring_copy(direction, 1, 2).start()
    ring_turn(2, (0, 1))
    ring_turn(1, (2,))
    ring_turn(3, (0, 1))
    ring_turn(2, (2,))
    ring_turn(4, (0, 1))

    def partners(half):
        return [
            (dz, dx)
            for dz in Z_ORDER
            for dx in X_ORDER[half * 2 : half * 2 + 2]
            if (dz, dx) != (0, 0)
        ]

    def up(half):
        span = slice(half * HALF, (half + 1) * HALF)
        for dz, dx in partners(half):
            disp_copy(-dz % NZ, -dx % NX).wait_recv()
        for n in range(FF // 256):
            at = slice(n * 256, (n + 1) * 256)
            gated = jnp.dot(
                received[span, :], weights[0, :, at], preferred_element_type=jnp.float32
            )
            raised = jnp.dot(
                received[span, :], weights[1, :, at], preferred_element_type=jnp.float32
            )
            hidden[span, at] = (gated / (1.0 + jnp.exp(-gated)) * raised).astype(jnp.bfloat16)

    def down(half, group):
        span = slice(half * HALF, (half + 1) * HALF)
        for n in range(*GROUPS[group]):
            rows = pl.ds(pl.multiple_of(ys[Y_ORDER[n]] * 256, 256), 256)
            produced[span, n * 256 : (n + 1) * 256] = lax.dot_general(
                hidden[span, :], weights[2, rows, :], (((1,), (1,)), ((), ())),
                preferred_element_type=jnp.float32,
            ).astype(jnp.bfloat16)

    def give_back(half, group):
        for dz, dx in partners(half):
            ret_copy(dz, dx, group).start()

    def give_back_by_z(group):
        for target in LAST_ORDER:
            dz = lax.rem(target - z + NZ, NZ)
            for dx in X_ORDER:
                copy = pltpu.make_async_remote_copy(
                    src_ref=produced.at[
                        pl.ds(pl.multiple_of((X_ORDER.index(dx) * NZ + dz) * CAP, CAP), CAP),
                        slice(256 * GROUPS[group][0], 256 * GROUPS[group][1]),
                    ],
                    dst_ref=returned.at[
                        pl.ds(
                            pl.multiple_of(
                                (lax.rem(NZ - dz, NZ) * NX + (-dx % NX)) * CAP, CAP
                            ),
                            CAP,
                        ),
                        slice(256 * GROUPS[group][0], 256 * GROUPS[group][1]),
                    ],
                    send_sem=ret_send.at[group, dz * NX + dx],
                    recv_sem=ret_recv.at[group, dz * NX + dx],
                    device_id=(grp, target * NX + xs[dx]), device_id_type=MESH,
                )
                if dx == 0:
                    pl.when(target != z)(copy.start)
                else:
                    copy.start()

    def sib_wait(m, kinds):
        for kind in kinds:
            sib_copy(kind, m, 1 - core).wait_recv()

    for load in loads[6:]:
        load.wait()
    for m in range(2):
        sib_wait(m, range(1 + NY))
    up(0)
    sib_wait(2, (0, 1, 2, 5, 6))
    down(0, 0)
    give_back(0, 0)
    ring_turn(3, (2,))
    up(1)
    down(1, 0)
    give_back(1, 0)
    ring_turn(4, (2,))
    sib_wait(2, (3, 4, 7, 8))
    down(0, 1)
    down(1, 1)
    give_back_by_z(1)

    returned[slots_of(0, 0), :] = produced[place_of(0, 0), :]

    for d in range(1, NZ):
        pz_copy(d, arrives=True).wait_recv()
    for d in range(1, NX):
        px_copy(d).start()
    for d in range(1, NX):
        px_copy(d, arrives=True).wait_recv()

    @pl.loop(0, NEP // 2)
    def _(i):
        first = prompt_buf[i // 4, (i % 4) * 2].astype(jnp.float32)
        second = prompt_buf[i // 4, (i % 4) * 2 + 1].astype(jnp.float32)
        at = pl.ds(pl.multiple_of(i * 2 * PROMPT_ROWS, 2 * PROMPT_ROWS), 2 * PROMPT_ROWS)
        keys[at, :] = jnp.concatenate(
            [first[:PROMPT_ROWS], second[:PROMPT_ROWS]], axis=0
        ).astype(jnp.bfloat16)
        values[at, :] = jnp.concatenate(
            [first[PROMPT_ROWS:], second[PROMPT_ROWS:]], axis=0
        ).astype(jnp.bfloat16)

    causal = lax.broadcasted_iota(jnp.int32, (TOK, TOK), 1) <= lax.broadcasted_iota(
        jnp.int32, (TOK, TOK), 0
    )
    loads[4].wait()
    loads[5].wait()

    @pl.loop(0, HQ, unroll=2)
    def _(head):
        at = pl.ds(pl.multiple_of(head * HD, HD), HD)
        kv = pl.ds(pl.multiple_of((head // (HQ // KVH)) * HD, HD), HD)
        kv_value = pl.ds(pl.multiple_of(KVH * HD + (head // (HQ // KVH)) * HD, HD), HD)
        query = q_buf[:, at]
        contract = (((1,), (1,)), ((), ()))
        shared = lax.dot_general(
            query, keys[:, kv], contract, preferred_element_type=jnp.float32
        )
        own = lax.dot_general(
            query, resp_kv[:, kv], contract, preferred_element_type=jnp.float32
        )
        own = jnp.where(causal, own, -jnp.inf)
        top = jnp.maximum(
            jnp.max(shared, axis=-1, keepdims=True), jnp.max(own, axis=-1, keepdims=True)
        )
        shared = jnp.exp((shared - top) * SCALE)
        own = jnp.exp((own - top) * SCALE)
        denominator = jnp.sum(shared, axis=-1, keepdims=True) + jnp.sum(
            own, axis=-1, keepdims=True
        )
        summed = jnp.dot(
            shared.astype(jnp.bfloat16), values[:, kv], preferred_element_type=jnp.float32
        ) + jnp.dot(
            own.astype(jnp.bfloat16), resp_kv[:, kv_value], preferred_element_type=jnp.float32
        )
        ctx_buf[:, at] = (summed / denominator).astype(jnp.bfloat16)

    ctx_copy = pltpu.make_async_copy(ctx_buf, ctx_hbm, local_sem.at[9])
    ctx_copy.start()

    for m in range(3):
        for direction in range(2):
            for step in range(1, NY // 2 + 1):
                ring_copy(direction, step, m).wait_send()
        for kind in range(1 + NY):
            sib_copy(kind, m, core).wait_send()
    for d in range(1, NZ):
        pz_copy(d).wait_send()
    for d in range(1, NX):
        px_copy(d).wait_send()
    for dz, dx in OFFSETS:
        disp_copy(dz, dx).wait_send()

    def moe_copy(n):
        columns = pl.ds(pl.multiple_of(ys[Y_ORDER[n]] * 256, 256), 256)
        return pltpu.make_async_copy(
            moe_out.at[:, n * 256 : (n + 1) * 256], moe_hbm_out.at[:, columns], local_sem.at[10 + n]
        )

    ctx_copy.wait()
    for group in range(len(GROUPS)):
        for dz, dx in OFFSETS:
            ret_copy(dz, dx, group).wait_send()
        for dz, dx in OFFSETS:
            ret_copy(dz, dx, group).wait_recv()
        for n in range(*GROUPS[group]):
            at = slice(n * 256, (n + 1) * 256)
            moe_out[:, at] = (
                jnp.dot(gate_hi[...], returned[:, at], preferred_element_type=jnp.float32)
                + jnp.dot(gate_lo[...], returned[:, at], preferred_element_type=jnp.float32)
            ).astype(jnp.bfloat16)
            moe_copy(n).start()
    for n in range(NY):
        moe_copy(n).wait()


def publish_kernel(ctx, moe, ctx_out, moe_out, ctx_buf, moe_buf, in_sem, out_sem):
    pieces = [(ctx, ctx_buf, ctx_out, i, TOK // 4) for i in range(4)]
    pieces += [(moe, moe_buf, moe_out, i, TOK // 2) for i in range(2)]
    incoming, outgoing = [], []
    for n, (src, buf, dst, i, rows) in enumerate(pieces):
        at = slice(i * rows, (i + 1) * rows)
        incoming.append(pltpu.make_async_copy(src.at[at], buf.at[at], in_sem.at[n]))
        outgoing.append(pltpu.make_async_copy(buf.at[at], dst.at[at], out_sem.at[n]))
    for copy in incoming:
        copy.start()
    for copy, following in zip(incoming, outgoing):
        copy.wait()
        following.start()
    for copy in outgoing:
        copy.wait()


def publish(ctx, moe):
    anywhere = pl.BlockSpec(memory_space=pl.ANY)
    return pl.pallas_call(
        publish_kernel,
        out_shape=tuple(jax.ShapeDtypeStruct(a.shape, a.dtype) for a in (ctx, moe)),
        in_specs=[anywhere] * 2,
        out_specs=(anywhere,) * 2,
        scratch_shapes=[
            pltpu.VMEM(ctx.shape, ctx.dtype),
            pltpu.VMEM(moe.shape, moe.dtype),
            pltpu.SemaphoreType.DMA((6,)),
            pltpu.SemaphoreType.DMA((6,)),
        ],
        compiler_params=pltpu.CompilerParams(vmem_limit_bytes=VMEM_LIMIT),
    )(ctx, moe)


def body(resp_q, resp_kv, prompt_kv, moe_in, routes, gate_probs, w_gate, w_up, w_down):
    anywhere = pl.BlockSpec(memory_space=pl.ANY)
    bf16 = jnp.bfloat16
    dma = pltpu.SemaphoreType.DMA
    results = pl.pallas_call(
        layer_kernel,
        out_shape=(
            jax.ShapeDtypeStruct((TOK, HQ * HD), bf16),
            jax.ShapeDtypeStruct((TOK, D), bf16),
        ),
        in_specs=[anywhere] * 9,
        out_specs=(anywhere, anywhere),
        scratch_shapes=[
            pltpu.VMEM((3, D, FF), bf16),
            pltpu.VMEM((SLOTS, D), bf16),
            pltpu.VMEM((SLOTS, D), bf16),
            pltpu.VMEM((SLOTS, FF), bf16),
            pltpu.VMEM((SLOTS, D), bf16),
            pltpu.VMEM((SLOTS, D), bf16),
            pltpu.VMEM((TOK, SLOTS), bf16),
            pltpu.VMEM((TOK, SLOTS), bf16),
            pltpu.VMEM((TOK, HQ * HD), bf16),
            pltpu.VMEM((TOK, HQ * HD), bf16),
            pltpu.VMEM((NX, NZ, 2 * PROMPT_ROWS, KVH * HD), bf16),
            pltpu.VMEM((NEP * PROMPT_ROWS, KVH * HD), bf16),
            pltpu.VMEM((NEP * PROMPT_ROWS, KVH * HD), bf16),
            pltpu.VMEM((TOK, 2 * KVH * HD), bf16),
            pltpu.VMEM((PROMPT_ROWS, 2 * KVH * HD), bf16),
            pltpu.VMEM((TOK, D), bf16),
            pltpu.VMEM((TOPK, TOK), jnp.int32),
            pltpu.VMEM((TOPK, TOK), jnp.float32),
            pltpu.VMEM((TOK, D), bf16),
            dma((10 + NY,)),
            dma((2, NY // 2, 3)),
            dma((2, NY // 2, 3)),
            dma((1 + NY, 3)),
            dma((1 + NY, 3)),
            dma((NZ - 1,)),
            dma((NZ - 1,)),
            dma((NX - 1,)),
            dma((NX - 1,)),
            dma((NEP,)),
            dma((NEP,)),
            dma((len(GROUPS), NEP)),
            dma((len(GROUPS), NEP)),
        ],
        compiler_params=pltpu.CompilerParams(
            collective_id=0, has_side_effects=True, vmem_limit_bytes=VMEM_LIMIT
        ),
        cost_estimate=pl.CostEstimate(
            flops=7_000_000_000, bytes_accessed=6_000_000, transcendentals=4_000_000
        ),
    )(
        resp_q, resp_kv, prompt_kv, moe_in, routes.T, gate_probs.T,
        w_gate[0], w_up[0], w_down[0],
    )
    return publish(*results)


def solution(mesh):
    placed = P(("grp", "ep"), None)
    weight = P("ep", "grp", None)
    return jax.shard_map(
        body,
        mesh=mesh,
        in_specs=(placed,) * 6 + (weight,) * 3,
        out_specs=(placed, placed),
        check_vma=False,
    )
```

```python
import jax
import jax.numpy as jnp
from jax import lax
from jax.experimental import pallas as pl
from jax.experimental.pallas import tpu as pltpu
from jax.sharding import PartitionSpec as P

D = 2048
FF = 768
HQ = 32
KVH = 2
HD = 128
TOPK = 8
TOK = 128
CAP = 16
EXP_DEV = 4
SHARD = 128
PROMPT_ROWS = 24
NX, NY, NZ = 4, 8, 8
NEP = NX * NZ
SLOTS = NEP * CAP
HALF = SLOTS // 2
MESH = pl.DeviceIdType.MESH
SCALE = HD ** -0.5
VMEM_LIMIT = 62 * 1024 * 1024


OFFSETS = [divmod(d, NX) for i in range(1, NEP // 2) for d in (i, NEP - i)] + [(NZ // 2, 0)]
Z_ORDER = (1, 7, 2, 6, 3, 5, 4, 0)
X_ORDER = (0, 2, 1, 3)
Y_ORDER = (0, 1, 7, 2, 6, 3, 5, 4)
GROUPS = ((0, 5), (5, 8))
LAST_ORDER = (0, 4, 1, 5, 2, 6, 3, 7)


def layer_kernel(
    q_hbm, resp_hbm, prompt_hbm, moe_hbm, routes_hbm, gates_hbm, wg_hbm, wu_hbm, wd_hbm,
    ctx_hbm, moe_out,
    weights, outgoing, received, hidden, produced, returned, gate_hi, gate_lo,
    q_buf, ctx_buf, prompt_buf, keys, values, resp_kv, prompt_kv, moe_in, routes_t, gates_t,
    local_sem, ring_send, ring_recv, sib_send, sib_recv, pz_send, pz_recv, px_send, px_recv,
    disp_send, disp_recv, ret_send, ret_recv,
):
    grp = lax.axis_index("grp")
    ep = lax.axis_index("ep")
    y, core = lax.div(grp, 2), lax.rem(grp, 2)
    z, x = lax.div(ep, NX), lax.rem(ep, NX)
    zs = [lax.rem(z + i, NZ) for i in range(NZ)]
    xs = [lax.rem(x + i, NX) for i in range(NX)]
    ys = [lax.rem(y + i, NY) for i in range(NY)]
    sibling = y * 2 + (1 - core)
    right = ys[1] * 2 + core
    left = ys[NY - 1] * 2 + core
    shards = (wg_hbm, wu_hbm, wd_hbm)

    def in_plane(dz, dx):
        return (grp, zs[dz] * NX + xs[dx])

    barrier = pltpu.get_barrier_semaphore()
    for dz, dx in reversed(OFFSETS):
        pl.semaphore_signal(barrier, inc=1, device_id=in_plane(dz, dx), device_id_type=MESH)
    for other in (sibling, right, left):
        pl.semaphore_signal(barrier, inc=1, device_id=(other, ep), device_id_type=MESH)

    loads = [
        pltpu.make_async_copy(src, dst, local_sem.at[i])
        for i, (src, dst) in enumerate(
            [
                (routes_hbm, routes_t), (moe_hbm, moe_in), (prompt_hbm, prompt_kv),
                (gates_hbm, gates_t), (q_hbm, q_buf), (resp_hbm, resp_kv),
            ]
            + [(shards[m], weights.at[m, pl.ds(grp * SHARD, SHARD), :]) for m in range(3)]
        )
    ]
    for load in loads[:4]:
        load.start()

    for load in loads[4:]:
        load.start()

    def shard_rows(origin):
        return pl.ds(pl.multiple_of(origin * SHARD, SHARD), SHARD)

    def ring_span(direction, step, m, of_core):
        origin = ys[(-step if direction == 0 else step) % NY] * 2 + of_core
        if step == NY // 2:
            start = pl.multiple_of(origin * SHARD + direction * (SHARD // 2), SHARD // 2)
            return weights.at[m, pl.ds(start, SHARD // 2), :]
        return weights.at[m, shard_rows(origin), :]

    def ring_copy(direction, step, m):
        dst = ring_span(direction, step - 1, m, core)
        if step == NY // 2:
            origin = ys[(1 - step if direction == 0 else step - 1) % NY] * 2 + core
            start = pl.multiple_of(origin * SHARD + direction * (SHARD // 2), SHARD // 2)
            dst = weights.at[m, pl.ds(start, SHARD // 2), :]
        return pltpu.make_async_remote_copy(
            src_ref=shards[m] if step == 1 else dst, dst_ref=dst,
            send_sem=ring_send.at[direction, step - 1, m],
            recv_sem=ring_recv.at[direction, step - 1, m],
            device_id=(right if direction == 0 else left, ep), device_id_type=MESH,
        )

    def ring_arrival(direction, step, m):
        landed = ring_span(direction, step, m, core)
        return pltpu.make_async_remote_copy(
            src_ref=landed, dst_ref=landed,
            send_sem=ring_send.at[direction, step - 1, m],
            recv_sem=ring_recv.at[direction, step - 1, m],
            device_id=(right if direction == 0 else left, ep), device_id_type=MESH,
        )

    def sib_copy(kind, m, of_core):
        if kind == 0:
            span = weights.at[m, shard_rows(y * 2 + of_core), :]
        else:
            span = ring_span((kind - 1) // (NY // 2), (kind - 1) % (NY // 2) + 1, m, of_core)
        return pltpu.make_async_remote_copy(
            src_ref=shards[m] if kind == 0 else span, dst_ref=span,
            send_sem=sib_send.at[kind, m], recv_sem=sib_recv.at[kind, m],
            device_id=(sibling, ep), device_id_type=MESH,
        )

    def pz_copy(d, arrives=False):
        block = prompt_buf.at[x, zs[-d % NZ] if arrives else z]
        return pltpu.make_async_remote_copy(
            src_ref=block, dst_ref=block, send_sem=pz_send.at[d - 1], recv_sem=pz_recv.at[d - 1],
            device_id=in_plane(d, 0), device_id_type=MESH,
        )

    def px_copy(d, arrives=False):
        block = prompt_buf.at[xs[-d % NX] if arrives else x]
        return pltpu.make_async_remote_copy(
            src_ref=block, dst_ref=block, send_sem=px_send.at[d - 1], recv_sem=px_recv.at[d - 1],
            device_id=in_plane(0, d), device_id_type=MESH,
        )

    def slots_of(dz, dx):
        at = (dz * NX + dx) * CAP
        return slice(at, at + CAP)

    def place_of(dz, dx):
        at = (X_ORDER.index(dx) * NZ + dz) * CAP
        return slice(at, at + CAP)

    def disp_copy(dz, dx):
        k = dz * NX + dx
        return pltpu.make_async_remote_copy(
            src_ref=outgoing.at[slots_of(dz, dx), :],
            dst_ref=received.at[place_of(-dz % NZ, -dx % NX), :],
            send_sem=disp_send.at[k], recv_sem=disp_recv.at[k],
            device_id=in_plane(dz, dx), device_id_type=MESH,
        )

    def ret_copy(dz, dx, group):
        k = dz * NX + dx
        columns = slice(256 * GROUPS[group][0], 256 * GROUPS[group][1])
        return pltpu.make_async_remote_copy(
            src_ref=produced.at[place_of(dz, dx), columns],
            dst_ref=returned.at[slots_of(-dz % NZ, -dx % NX), columns],
            send_sem=ret_send.at[group, k], recv_sem=ret_recv.at[group, k],
            device_id=in_plane(dz, dx), device_id_type=MESH,
        )

    row = lax.broadcasted_iota(jnp.int32, (NEP, TOK), 0)
    owner_z, owner_x = (z + row // NX) % NZ, (x + row % NX) % NX
    owner_expert = (owner_z * NX + owner_x) * EXP_DEV
    loads[0].wait()
    member = jnp.zeros((NEP, TOK), jnp.float32)
    for k in range(TOPK):
        member = member + jnp.where(routes_t[k : k + 1, :] == owner_expert, 1.0, 0.0)
    earlier = lax.broadcasted_iota(jnp.int32, (TOK, TOK), 0) < lax.broadcasted_iota(
        jnp.int32, (TOK, TOK), 1
    )
    position = jnp.dot(
        member.astype(jnp.bfloat16),
        jnp.where(earlier, 1.0, 0.0).astype(jnp.bfloat16),
        preferred_element_type=jnp.float32,
    )
    position = jnp.where(member > 0.0, position, -1.0)
    slot = lax.broadcasted_iota(jnp.int32, (NEP, CAP, TOK), 1).astype(jnp.float32)
    taken = jnp.broadcast_to(position[:, None, :], (NEP, CAP, TOK)) == slot
    onehot = jnp.where(taken, 1.0, 0.0).reshape(SLOTS, TOK).astype(jnp.bfloat16)
    loads[1].wait()
    for n in range(D // 256):
        outgoing[:, n * 256 : (n + 1) * 256] = jnp.dot(
            onehot, moe_in[:, n * 256 : (n + 1) * 256], preferred_element_type=jnp.float32
        ).astype(jnp.bfloat16)

    loads[2].wait()
    rows = prompt_kv[...].astype(jnp.float32)
    prompt_buf[x, z] = jnp.concatenate(
        [rows[:, : KVH * HD], rows[:, KVH * HD :]], axis=0
    ).astype(jnp.bfloat16)

    pl.semaphore_wait(barrier, NEP + 2)
    for m in range(2):
        for direction in range(2):
            ring_copy(direction, 1, m).start()
    for half in range(2):
        for dz, dx in OFFSETS:
            if dx in X_ORDER[half * 2 : half * 2 + 2]:
                disp_copy(dz, dx).start()
    for d in range(1, NZ):
        pz_copy(d).start()
    for m in range(3):
        sib_copy(0, m, core).start()

    received[place_of(0, 0), :] = outgoing[slots_of(0, 0), :]

    loads[3].wait()
    gate = jnp.zeros((NEP, TOK), jnp.float32)
    for k in range(TOPK):
        hit = routes_t[k : k + 1, :] == owner_expert
        gate = gate + jnp.where(hit, gates_t[k : k + 1, :], 0.0)
    spread = jnp.where(taken, jnp.broadcast_to(gate[:, None, :], (NEP, CAP, TOK)), 0.0)
    spread = spread.reshape(SLOTS, TOK).T
    high = spread.astype(jnp.bfloat16)
    gate_hi[...] = high
    gate_lo[...] = (spread - high.astype(jnp.float32)).astype(jnp.bfloat16)

    def ring_turn(step, matrices):
        for m in matrices:
            for direction in range(2):
                ring_arrival(direction, step, m).wait_recv()
                if step < NY // 2:
                    ring_copy(direction, step + 1, m).start()
                sib_copy(1 + direction * (NY // 2) + step - 1, m, core).start()

    ring_turn(1, (0, 1))
    for direction in range(2):
        ring_copy(direction, 1, 2).start()
    ring_turn(2, (0, 1))
    ring_turn(1, (2,))
    ring_turn(3, (0, 1))
    ring_turn(2, (2,))
    ring_turn(4, (0, 1))

    def partners(half):
        return [
            (dz, dx)
            for dz in Z_ORDER
            for dx in X_ORDER[half * 2 : half * 2 + 2]
            if (dz, dx) != (0, 0)
        ]

    def up(half):
        span = slice(half * HALF, (half + 1) * HALF)
        for dz, dx in partners(half):
            disp_copy(-dz % NZ, -dx % NX).wait_recv()
        for n in range(FF // 256):
            at = slice(n * 256, (n + 1) * 256)
            gated = jnp.dot(
                received[span, :], weights[0, :, at], preferred_element_type=jnp.float32
            )
            raised = jnp.dot(
                received[span, :], weights[1, :, at], preferred_element_type=jnp.float32
            )
            hidden[span, at] = (gated / (1.0 + jnp.exp(-gated)) * raised).astype(jnp.bfloat16)

    def down(half, group):
        span = slice(half * HALF, (half + 1) * HALF)
        for n in range(*GROUPS[group]):
            rows = pl.ds(pl.multiple_of(ys[Y_ORDER[n]] * 256, 256), 256)
            produced[span, n * 256 : (n + 1) * 256] = lax.dot_general(
                hidden[span, :], weights[2, rows, :], (((1,), (1,)), ((), ())),
                preferred_element_type=jnp.float32,
            ).astype(jnp.bfloat16)

    def give_back(half, group):
        for dz, dx in partners(half):
            ret_copy(dz, dx, group).start()

    def give_back_by_z(group):
        for target in LAST_ORDER:
            dz = lax.rem(target - z + NZ, NZ)
            for dx in X_ORDER:
                copy = pltpu.make_async_remote_copy(
                    src_ref=produced.at[
                        pl.ds(pl.multiple_of((X_ORDER.index(dx) * NZ + dz) * CAP, CAP), CAP),
                        slice(256 * GROUPS[group][0], 256 * GROUPS[group][1]),
                    ],
                    dst_ref=returned.at[
                        pl.ds(
                            pl.multiple_of(
                                (lax.rem(NZ - dz, NZ) * NX + (-dx % NX)) * CAP, CAP
                            ),
                            CAP,
                        ),
                        slice(256 * GROUPS[group][0], 256 * GROUPS[group][1]),
                    ],
                    send_sem=ret_send.at[group, dz * NX + dx],
                    recv_sem=ret_recv.at[group, dz * NX + dx],
                    device_id=(grp, target * NX + xs[dx]), device_id_type=MESH,
                )
                if dx == 0:
                    pl.when(target != z)(copy.start)
                else:
                    copy.start()

    def sib_wait(m, kinds):
        for kind in kinds:
            sib_copy(kind, m, 1 - core).wait_recv()

    for load in loads[6:]:
        load.wait()
    for m in range(2):
        sib_wait(m, range(1 + NY))
    up(0)
    sib_wait(2, (0, 1, 2, 5, 6))
    down(0, 0)
    give_back(0, 0)
    ring_turn(3, (2,))
    up(1)
    down(1, 0)
    give_back(1, 0)
    ring_turn(4, (2,))
    sib_wait(2, (3, 4, 7, 8))
    down(0, 1)
    down(1, 1)
    give_back_by_z(1)

    returned[slots_of(0, 0), :] = produced[place_of(0, 0), :]

    for d in range(1, NZ):
        pz_copy(d, arrives=True).wait_recv()
    for d in range(1, NX):
        px_copy(d).start()
    for d in range(1, NX):
        px_copy(d, arrives=True).wait_recv()

    @pl.loop(0, NEP // 2)
    def _(i):
        first = prompt_buf[i // 4, (i % 4) * 2].astype(jnp.float32)
        second = prompt_buf[i // 4, (i % 4) * 2 + 1].astype(jnp.float32)
        at = pl.ds(pl.multiple_of(i * 2 * PROMPT_ROWS, 2 * PROMPT_ROWS), 2 * PROMPT_ROWS)
        keys[at, :] = jnp.concatenate(
            [first[:PROMPT_ROWS], second[:PROMPT_ROWS]], axis=0
        ).astype(jnp.bfloat16)
        values[at, :] = jnp.concatenate(
            [first[PROMPT_ROWS:], second[PROMPT_ROWS:]], axis=0
        ).astype(jnp.bfloat16)

    causal = lax.broadcasted_iota(jnp.int32, (TOK, TOK), 1) <= lax.broadcasted_iota(
        jnp.int32, (TOK, TOK), 0
    )
    loads[4].wait()
    loads[5].wait()

    @pl.loop(0, HQ, unroll=2)
    def _(head):
        at = pl.ds(pl.multiple_of(head * HD, HD), HD)
        kv = pl.ds(pl.multiple_of((head // (HQ // KVH)) * HD, HD), HD)
        kv_value = pl.ds(pl.multiple_of(KVH * HD + (head // (HQ // KVH)) * HD, HD), HD)
        query = q_buf[:, at]
        contract = (((1,), (1,)), ((), ()))
        shared = lax.dot_general(
            query, keys[:, kv], contract, preferred_element_type=jnp.float32
        )
        own = lax.dot_general(
            query, resp_kv[:, kv], contract, preferred_element_type=jnp.float32
        )
        own = jnp.where(causal, own, -jnp.inf)
        top = jnp.maximum(
            jnp.max(shared, axis=-1, keepdims=True), jnp.max(own, axis=-1, keepdims=True)
        )
        shared = jnp.exp((shared - top) * SCALE)
        own = jnp.exp((own - top) * SCALE)
        denominator = jnp.sum(shared, axis=-1, keepdims=True) + jnp.sum(
            own, axis=-1, keepdims=True
        )
        summed = jnp.dot(
            shared.astype(jnp.bfloat16), values[:, kv], preferred_element_type=jnp.float32
        ) + jnp.dot(
            own.astype(jnp.bfloat16), resp_kv[:, kv_value], preferred_element_type=jnp.float32
        )
        ctx_buf[:, at] = (summed / denominator).astype(jnp.bfloat16)

    ctx_copy = pltpu.make_async_copy(ctx_buf, ctx_hbm, local_sem.at[9])
    ctx_copy.start()

    for m in range(3):
        for direction in range(2):
            for step in range(1, NY // 2 + 1):
                ring_copy(direction, step, m).wait_send()
        for kind in range(1 + NY):
            sib_copy(kind, m, core).wait_send()
    for d in range(1, NZ):
        pz_copy(d).wait_send()
    for d in range(1, NX):
        px_copy(d).wait_send()
    for dz, dx in OFFSETS:
        disp_copy(dz, dx).wait_send()

    ctx_copy.wait()
    for group in range(len(GROUPS)):
        for dz, dx in OFFSETS:
            ret_copy(dz, dx, group).wait_send()
        for dz, dx in OFFSETS:
            ret_copy(dz, dx, group).wait_recv()
        for n in range(*GROUPS[group]):
            at = slice(n * 256, (n + 1) * 256)
            columns = pl.ds(pl.multiple_of(ys[Y_ORDER[n]] * 256, 256), 256)
            moe_out[:, columns] = (
                jnp.dot(gate_hi[...], returned[:, at], preferred_element_type=jnp.float32)
                + jnp.dot(gate_lo[...], returned[:, at], preferred_element_type=jnp.float32)
            ).astype(jnp.bfloat16)


def publish_kernel(ctx, moe, ctx_out, moe_out, ctx_buf, moe_buf, in_sem, out_sem):
    pieces = [(ctx, ctx_buf, ctx_out, i, TOK // 4) for i in range(4)]
    pieces += [(moe, moe_buf, moe_out, i, TOK // 2) for i in range(2)]
    incoming, outgoing = [], []
    for n, (src, buf, dst, i, rows) in enumerate(pieces):
        at = slice(i * rows, (i + 1) * rows)
        incoming.append(pltpu.make_async_copy(src.at[at], buf.at[at], in_sem.at[n]))
        outgoing.append(pltpu.make_async_copy(buf.at[at], dst.at[at], out_sem.at[n]))
    for copy in incoming:
        copy.start()
    for copy, following in zip(incoming, outgoing):
        copy.wait()
        following.start()
    for copy in outgoing:
        copy.wait()


def publish(ctx, moe):
    anywhere = pl.BlockSpec(memory_space=pl.ANY)
    return pl.pallas_call(
        publish_kernel,
        out_shape=tuple(jax.ShapeDtypeStruct(a.shape, a.dtype) for a in (ctx, moe)),
        in_specs=[anywhere] * 2,
        out_specs=(anywhere,) * 2,
        scratch_shapes=[
            pltpu.VMEM(ctx.shape, ctx.dtype),
            pltpu.VMEM(moe.shape, moe.dtype),
            pltpu.SemaphoreType.DMA((6,)),
            pltpu.SemaphoreType.DMA((6,)),
        ],
        compiler_params=pltpu.CompilerParams(vmem_limit_bytes=VMEM_LIMIT),
    )(ctx, moe)


def body(resp_q, resp_kv, prompt_kv, moe_in, routes, gate_probs, w_gate, w_up, w_down):
    vmem = pl.BlockSpec(memory_space=pltpu.VMEM)
    anywhere = pl.BlockSpec(memory_space=pl.ANY)
    bf16 = jnp.bfloat16
    dma = pltpu.SemaphoreType.DMA
    results = pl.pallas_call(
        layer_kernel,
        out_shape=(
            jax.ShapeDtypeStruct((TOK, HQ * HD), bf16),
            jax.ShapeDtypeStruct((TOK, D), bf16),
        ),
        in_specs=[anywhere] * 9,
        out_specs=(anywhere, vmem),
        scratch_shapes=[
            pltpu.VMEM((3, D, FF), bf16),
            pltpu.VMEM((SLOTS, D), bf16),
            pltpu.VMEM((SLOTS, D), bf16),
            pltpu.VMEM((SLOTS, FF), bf16),
            pltpu.VMEM((SLOTS, D), bf16),
            pltpu.VMEM((SLOTS, D), bf16),
            pltpu.VMEM((TOK, SLOTS), bf16),
            pltpu.VMEM((TOK, SLOTS), bf16),
            pltpu.VMEM((TOK, HQ * HD), bf16),
            pltpu.VMEM((TOK, HQ * HD), bf16),
            pltpu.VMEM((NX, NZ, 2 * PROMPT_ROWS, KVH * HD), bf16),
            pltpu.VMEM((NEP * PROMPT_ROWS, KVH * HD), bf16),
            pltpu.VMEM((NEP * PROMPT_ROWS, KVH * HD), bf16),
            pltpu.VMEM((TOK, 2 * KVH * HD), bf16),
            pltpu.VMEM((PROMPT_ROWS, 2 * KVH * HD), bf16),
            pltpu.VMEM((TOK, D), bf16),
            pltpu.VMEM((TOPK, TOK), jnp.int32),
            pltpu.VMEM((TOPK, TOK), jnp.float32),
            dma((10,)),
            dma((2, NY // 2, 3)),
            dma((2, NY // 2, 3)),
            dma((1 + NY, 3)),
            dma((1 + NY, 3)),
            dma((NZ - 1,)),
            dma((NZ - 1,)),
            dma((NX - 1,)),
            dma((NX - 1,)),
            dma((NEP,)),
            dma((NEP,)),
            dma((len(GROUPS), NEP)),
            dma((len(GROUPS), NEP)),
        ],
        compiler_params=pltpu.CompilerParams(
            collective_id=0, has_side_effects=True, vmem_limit_bytes=VMEM_LIMIT
        ),
        cost_estimate=pl.CostEstimate(
            flops=7_000_000_000, bytes_accessed=6_000_000, transcendentals=4_000_000
        ),
    )(
        resp_q, resp_kv, prompt_kv, moe_in, routes.T, gate_probs.T,
        w_gate[0], w_up[0], w_down[0],
    )
    return publish(*results)


def solution(mesh):
    placed = P(("grp", "ep"), None)
    weight = P("ep", "grp", None)
    return jax.shard_map(
        body,
        mesh=mesh,
        in_specs=(placed,) * 6 + (weight,) * 3,
        out_specs=(placed, placed),
        check_vma=False,
    )
```
